32 devices in a mesh: pairs: 8 (over y, x, core), aux: 4 (over z).
Axes of the slice: x: 2, y: 2, z: 4, core: 2. Of those that a mesh axis runs over, the one named last changes fastest.
Arguments:
- pair_orbits: int32 [512, 2], P('pairs'), may hold values from 0 to 255
- pno_count: int32 [512], P('pairs'), may hold values from 64 to 128
- partner: int32 [512, 12], P('pairs', 'aux'), may hold values from -1 to 511, as said below
- couple_orbit: int32 [512, 12], P('pairs', 'aux'), may hold values from 0 to 255
- couple_side: int32 [512, 12], P('pairs', 'aux'), may hold values from 0 to 1
- occ_fock: float32 [256, 256], replicated, may hold values from -2 to 1, as said below
- fit_left: bfloat16 [512, 128, 2048], P('pairs', None, 'aux'), may hold values from -0.8984375 to 0.8984375
- fit_right: bfloat16 [512, 128, 2048], P('pairs', None, 'aux'), may hold values from -0.8984375 to 0.8984375
- pno_coef: bfloat16 [512, 256, 128], P('pairs'), may hold values from -0.375 to 0.375
- virt_fock: bfloat16 [512, 128, 128], P('pairs'), may hold values from -0.25 to 3, as said below
- amps_in: float32 [512, 128, 128], P('pairs', 'aux'), may hold values from -1.8 to 1.8
Outputs:
- amps_out: float32 [512, 128, 128], P('pairs', 'aux')
The draws below stay inside these ranges and needn't reach their ends.
Inputs may be any that keep to these rules, and one draw needn't show every extreme that they name: partner[p, c] is -1 (no coupling) or a pair held by another index of pairs; couplings are mutual: if slot c of p names q then slot c of q names p. In each slot, the pairs of one index of pairs name pairs of one other index at most 2 times, and 2 is reached in every slot. `occ_fock`: symmetric; its diagonal lies between -2 and -0.3. `virt_fock`: symmetric in its last two dimensions; its diagonal lies between 0.5 and 3.
All inputs are finite; a program needn't handle non-finite values.
Results may differ from the reference program's by a relative error of at most 0.0019.
Values may be sent and summed in bfloat16 or wider, within the bound.
No kernel may reach another device: no remote copies, remote signals or barrier semaphores. Data moves between devices by JAX's collectives and lax.ppermute only.
A program may use at most 192 MiB of HBM per device.

```python
import jax
import jax.numpy as jnp
from jax import lax

NPNO = 128
NAUX = 2048
NV = 256
NOCC = 256
PAIR_DEV = 64
MOST = 2
ITERS = 2
COUPLE = 12
PAIRS = 512


def draw_partner(key, part):
    dev_count = PAIRS // PAIR_DEV
    device_ids = jnp.arange(dev_count, dtype=jnp.int32)
    level_raw = jax.random.randint(jax.random.fold_in(key, 7), (dev_count,), 0, 10)
    device_level = (level_raw >= 4).astype(jnp.int32) + (level_raw >= 7).astype(jnp.int32)
    device_level = jnp.minimum(device_level, MOST)
    position = jnp.arange(PAIR_DEV, dtype=jnp.int32)
    columns = []
    for slot_id in range(COUPLE):
        slot_key = jax.random.fold_in(key, 100 + slot_id)
        key_first, key_second, key_order = jax.random.split(slot_key, 3)
        pair_count = jnp.minimum(device_level[:, None], device_level[None, :])
        first_dev = jax.random.randint(key_first, (), 0, dev_count)
        second_dev = (first_dev + 1 + jax.random.randint(key_second, (), 0, dev_count - 1)) % dev_count
        forced = (device_ids[:, None] == first_dev) & (device_ids[None, :] == second_dev) | (device_ids[:, None] == second_dev) & (device_ids[None, :] == first_dev)
        pair_count = jnp.where(forced, MOST, pair_count)
        pair_count = jnp.where(device_ids[:, None] == device_ids[None, :], 0, pair_count)
        block_ends = jnp.cumsum(pair_count, axis=1)
        block_starts = block_ends - pair_count
        orders = jax.vmap(lambda sub_key: jax.random.permutation(sub_key, PAIR_DEV))(jax.random.split(key_order, dev_count)).astype(jnp.int32)
        peer_index = jnp.sum((block_ends[:, None, :] <= position[None, :, None]).astype(jnp.int32), axis=2)
        is_live = peer_index < dev_count
        peer_safe = jnp.minimum(peer_index, dev_count - 1)
        offset = position[None, :] - jnp.take_along_axis(block_starts, peer_safe, axis=1)
        back_start = block_starts[peer_safe, device_ids[:, None]]
        far_spot = jnp.clip(back_start + offset, 0, PAIR_DEV - 1)
        far_local = orders[peer_safe, far_spot]
        partner_value = jnp.where(is_live, peer_safe * PAIR_DEV + far_local, -1)
        result = jnp.full((dev_count, PAIR_DEV), -1, jnp.int32).at[device_ids[:, None], orders].set(partner_value.astype(jnp.int32))
        columns.append(result.reshape(-1))
    return jnp.stack(columns, axis=1).astype(jnp.int32)


def draw_occ_fock(key, part):
    key_off, key_diag = jax.random.split(jax.random.fold_in(key, 11))
    raw_part = 0.15 * jax.random.normal(key_off, (NOCC, NOCC), jnp.float32)
    coupled = jnp.clip(raw_part + raw_part.T, -1.0, 1.0)
    energies = jax.random.uniform(key_diag, (NOCC,), jnp.float32, -2.0, -0.3)
    eye_mask = jnp.eye(NOCC, dtype=jnp.float32)
    return (coupled * (1.0 - eye_mask) + eye_mask * energies[None, :]).astype(jnp.float32)


def draw_virt_fock(key, part):
    key_off, key_diag = jax.random.split(jax.random.fold_in(key, 13))
    raw_part = 0.03 * jax.random.normal(key_off, (PAIRS, NPNO, NPNO), jnp.float32)
    coupled = jnp.clip(raw_part + jnp.swapaxes(raw_part, 1, 2), -0.25, 0.25)
    energies = jax.random.uniform(key_diag, (PAIRS, NPNO), jnp.float32, 0.5, 3.0)
    eye_mask = jnp.eye(NPNO, dtype=jnp.float32)
    whole = coupled * (1.0 - eye_mask[None, :, :]) + eye_mask[None, :, :] * energies[:, :, None]
    return whole.astype(jnp.bfloat16)


def with_ends(values, rng, smallest, high):
    place = [jax.random.randint(jax.random.fold_in(rng, axis), (), 0, length) for axis, length in enumerate(values.shape)]
    longest = values.shape.index(max(values.shape))
    neighbour = place[:longest] + [(place[longest] + 1) % values.shape[longest]] + place[longest + 1:]
    return values.at[tuple(place)].set(smallest).at[tuple(neighbour)].set(high)


def shard_levels(key, extent, cuts, low, top_value):
    def one(dim, blocks):
        draws = jax.random.uniform(jax.random.fold_in(jax.random.fold_in(key, 6), dim), (blocks,), jnp.float32, low / len(cuts), top_value / len(cuts))
        return jnp.repeat(jnp.exp(draws), extent[dim] // blocks).reshape((-1,) + (1,) * (len(extent) - dim - 1))

    loudness = one(*cuts[0])
    for cut in cuts[1:]:
        loudness = loudness * one(*cut)
    return loudness


def scatter_about(own_key, shape, spread, limit, cuts=(), held_as=jnp.bfloat16):
    values = jax.random.normal(own_key, shape, jnp.float32) * spread
    if len(cuts) > 0:
        values = shard_levels(own_key, shape, cuts, -0.22, 0.18) * values
    return jnp.clip(values, min=-limit, max=limit).astype(held_as)


def setup_inputs(seed: int = 0) -> dict:
    key_of = jax.random.split(jax.random.key(seed), 12)
    return {
        "pair_orbits": with_ends(jax.random.randint(key_of[0], (PAIRS, 2), 0, NOCC), jax.random.fold_in(key_of[0], 1), 0, NOCC - 1).astype(jnp.int32),
        "pno_count": with_ends(jax.random.randint(key_of[1], (PAIRS,), NPNO // 2, NPNO + 1), jax.random.fold_in(key_of[1], 1), NPNO // 2, NPNO).astype(jnp.int32),
        "partner": draw_partner(jax.random.fold_in(key_of[11], 71), 0),
        "couple_orbit": with_ends(jax.random.randint(key_of[3], (PAIRS, COUPLE), 0, NOCC), jax.random.fold_in(key_of[3], 1), 0, NOCC - 1).astype(jnp.int32),
        "couple_side": with_ends(jax.random.randint(key_of[4], (PAIRS, COUPLE), 0, 2), jax.random.fold_in(key_of[4], 1), 0, 1).astype(jnp.int32),
        "occ_fock": draw_occ_fock(jax.random.fold_in(key_of[11], 71), 0),
        "fit_left": scatter_about(key_of[6], (PAIRS, NPNO, NAUX), 0.15, 0.8984375, ((0, 8), (2, 4))),
        "fit_right": scatter_about(key_of[7], (PAIRS, NPNO, NAUX), 0.15, 0.8984375, ((0, 8), (2, 4))),
        "pno_coef": scatter_about(key_of[8], (PAIRS, NV, NPNO), NV ** -0.5, 0.375, ((0, 8),)),
        "virt_fock": draw_virt_fock(jax.random.fold_in(key_of[11], 71), 0),
        "amps_in": scatter_about(key_of[10], (PAIRS, NPNO, NPNO), 0.3, 1.8, ((0, 8), (1, 4)), jnp.float32),
    }


def to_half(values):
    return lax.optimization_barrier(values.astype(jnp.bfloat16)).astype(jnp.float32)


def block_integrals(block_index, fit_left, fit_right):
    block_start = (block_index * PAIR_DEV).astype(jnp.int32)
    left_block = lax.dynamic_slice_in_dim(fit_left, block_start, PAIR_DEV, 0).astype(jnp.float32)
    right_block = lax.dynamic_slice_in_dim(fit_right, block_start, PAIR_DEV, 0).astype(jnp.float32)
    return jnp.einsum('pax,pbx->pab', left_block, right_block)


def block_coupling(block_index, partner, weight, pno_coef, amps_half):
    block_start = (block_index * PAIR_DEV).astype(jnp.int32)
    own_coef = lax.dynamic_slice_in_dim(pno_coef, block_start, PAIR_DEV, 0).astype(jnp.float32)
    partner_block = lax.dynamic_slice_in_dim(partner, block_start, PAIR_DEV, 0)
    weight_block = lax.dynamic_slice_in_dim(weight, block_start, PAIR_DEV, 0)
    pno_width = amps_half.shape[1]
    coupling = jnp.zeros((PAIR_DEV, pno_width, pno_width), jnp.float32)
    for slot_id in range(partner_block.shape[1]):
        target = partner_block[:, slot_id]
        safe_target = jnp.maximum(target, 0).astype(jnp.int32)
        far_coef = pno_coef[safe_target].astype(jnp.float32)
        projector = to_half(jnp.einsum('pvn,pvm->pnm', own_coef, far_coef))
        far_amps = amps_half[safe_target].astype(jnp.float32)
        mixed_amp = to_half(jnp.einsum('pab,pbc->pac', projector, far_amps))
        image = jnp.einsum('pac,pdc->pad', mixed_amp, projector)
        coupling = coupling + weight_block[:, slot_id][:, None, None] * image
    return coupling


def reference(pair_orbits, pno_count, partner, couple_orbit, couple_side, occ_fock, fit_left, fit_right, pno_coef, virt_fock, amps_in):
    pair_total = pno_count.shape[0]
    pno_width = virt_fock.shape[1]
    blocks = pair_total // PAIR_DEV
    block_ids = jnp.arange(blocks, dtype=jnp.int32)
    orbit_ids = jnp.arange(pno_width, dtype=jnp.int32)
    keep_vec = (orbit_ids[None, :] < pno_count[:, None]).astype(jnp.float32)
    keep_mask = keep_vec[:, :, None] * keep_vec[:, None, :]
    fock_diag = jnp.diagonal(virt_fock, axis1=1, axis2=2).astype(jnp.float32)
    occ_diag = jnp.diagonal(occ_fock)
    occ_energy = occ_diag[pair_orbits[:, 0]] + occ_diag[pair_orbits[:, 1]]
    denominator = fock_diag[:, :, None] + fock_diag[:, None, :] - occ_energy[:, None, None]
    free_orbit = jnp.where(couple_side == 0, pair_orbits[:, 0:1], pair_orbits[:, 1:2])
    weight = -occ_fock[couple_orbit, free_orbit]
    weight = jnp.where(partner >= 0, weight, jnp.zeros_like(weight))
    integrals = lax.map(lambda block_index: block_integrals(block_index, fit_left, fit_right), block_ids)
    integrals = integrals.reshape(pair_total, pno_width, pno_width)
    fock_full = virt_fock.astype(jnp.float32)
    amplitudes = amps_in * keep_mask
    for update in range(ITERS):
        amps_half = amplitudes.astype(jnp.bfloat16)
        coupling = lax.map(lambda block_index: block_coupling(block_index, partner, weight, pno_coef, amps_half), block_ids)
        coupling = coupling.reshape(pair_total, pno_width, pno_width)
        amps_wide = to_half(amplitudes)
        left_term = jnp.einsum('pab,pbc->pac', fock_full, amps_wide)
        right_term = jnp.einsum('pab,pbc->pac', amps_wide, fock_full)
        residual = integrals + left_term + right_term - occ_energy[:, None, None] * amplitudes + coupling
        amplitudes = (amplitudes - residual / denominator) * keep_mask
    return amplitudes
```

```python
import functools

import jax
import jax.numpy as jnp
from jax import lax
from jax.experimental import pallas as pl
from jax.experimental.pallas import tpu as pltpu
from jax.sharding import PartitionSpec as P

MOST = 2
VMEM_BYTES = 48 * 1024 * 1024

SMEM = pl.BlockSpec(memory_space=pltpu.SMEM)
VMEM = pl.BlockSpec(memory_space=pltpu.VMEM)
ANY = pl.BlockSpec(memory_space=pl.ANY)
HBM = pl.BlockSpec(memory_space=pltpu.HBM)
precise = lax.Precision.HIGHEST


def dot(left, right, over_left, over_right):
    return lax.dot_general(
        left, right, (((over_left,), (over_right,)), ((), ())), preferred_element_type=jnp.float32
    )


def params():
    return pltpu.CompilerParams(vmem_limit_bytes=VMEM_BYTES)


def pair_places(partner, pair_dev, dev_count):
    slots = partner.shape[1]
    owner = jnp.where(partner >= 0, partner // pair_dev, -1)
    own_id = jnp.broadcast_to(jnp.arange(pair_dev, dtype=jnp.int32)[:, None], partner.shape)
    far_key = (partner - owner * pair_dev) * pair_dev + own_id
    none = pair_dev * pair_dev
    devs = jnp.arange(dev_count, dtype=jnp.int32)[None, :, None]
    hit = owner[:, None, :] == devs

    def ranked(key):
        left = jnp.where(hit, key[:, None, :], none)
        found = []
        for _ in range(MOST):
            least = jnp.min(left, axis=0)
            found.append(least)
            left = jnp.where(left == least[None], none, left)
        return jnp.stack(found, axis=-1).reshape(-1)

    send = ranked(own_id)
    read = ranked(far_key)
    send = jnp.where(send < none, send, 0)
    read = jnp.where(read < none, lax.rem(read, pair_dev), -1)
    return send, read


def pack_rows(send_ref, half_ref, out_ref):
    def body(item, carry):
        out_ref[item] = half_ref[send_ref[item]]
        return carry

    lax.fori_loop(0, out_ref.shape[0], body, 0, unroll=4)


def start_kernel(place_ref, send_ref, count_ref, amps_ref, kept_ref, half_ref, out_ref):
    pairs, rows, width = amps_ref.shape
    row_id = lax.broadcasted_iota(jnp.int32, (rows, width), 0) + place_ref[1] * rows
    col_id = lax.broadcasted_iota(jnp.int32, (rows, width), 1)
    last = jnp.maximum(row_id, col_id)

    def body(pair, carry):
        kept = jnp.where(last < count_ref[pair], amps_ref[pair], 0.0)
        kept_ref[pair] = kept
        half_ref[pair] = kept.astype(jnp.bfloat16)
        return carry

    lax.fori_loop(0, pairs, body, 0, unroll=4)
    pack_rows(send_ref, half_ref, out_ref)


def coef_kernel(slots, place_ref, send_ref, coef_ref, *rest):
    outs, (held, in_sems, out_sems) = rest[:-3], rest[-3:]
    per_dev = slots * MOST

    def fetch(turn, item):
        far = place_ref[0] ^ (turn + 1)
        pair = send_ref[far * per_dev + item]
        place = turn * per_dev + item
        return pltpu.make_async_copy(coef_ref.at[pair], held.at[place], in_sems.at[place])

    def store(turn):
        return pltpu.make_async_copy(
            held.at[pl.ds(turn * per_dev, per_dev)], outs[turn], out_sems.at[turn]
        )

    for turn in range(len(outs)):
        for item in range(per_dev):
            fetch(turn, item).start()
    for turn in range(len(outs)):
        for item in range(per_dev):
            fetch(turn, item).wait()
        store(turn).start()
    for turn in range(len(outs)):
        store(turn).wait()


def left_part(fock_rows, half_rows):
    return dot(fock_rows, half_rows, 0, 0)


def prepare_kernel(
    place_ref, count_ref, energy_ref, left_ref, right_ref, fock_ref, kept_ref, half_ref,
    part_ref, scale_ref, own_ref,
):
    block, rows, width = kept_ref.shape
    first = pl.program_id(0) * block
    row_start = pl.multiple_of(place_ref[1] * rows, rows)
    row_id = lax.broadcasted_iota(jnp.int32, (rows, width), 0) + row_start
    col_id = lax.broadcasted_iota(jnp.int32, (rows, width), 1)
    last = jnp.maximum(row_id, col_id)
    eye_rows = row_id == col_id
    eye = lax.broadcasted_iota(jnp.int32, (width, width), 0) == lax.broadcasted_iota(
        jnp.int32, (width, width), 1
    )
    for pair in range(block):
        energy = energy_ref[first + pair]
        fock = fock_ref[pair]
        fock_rows = fock_ref[pair, pl.ds(row_start, rows), :]
        half = half_ref[pair]
        part_ref[pair] = dot(left_ref[pair], right_ref[pair], 1, 1) + left_part(fock_rows, half)
        own_ref[pair] = dot(half, fock, 1, 0) - energy * kept_ref[pair]
        diag_cols = jnp.sum(jnp.where(eye, fock.astype(jnp.float32), 0.0), axis=0, keepdims=True)
        diag_rows = jnp.sum(
            jnp.where(eye_rows, fock_rows.astype(jnp.float32), 0.0), axis=1, keepdims=True
        )
        denominator = diag_rows + diag_cols - energy
        scale_ref[pair] = jnp.where(last < count_ref[first + pair], 1.0 / denominator, 0.0)


def projector_kernel(slots, place_ref, read_ref, coef_ref, *rest):
    arrived, out_ref = rest[:-1], rest[-1]
    per_dev = slots * MOST
    for turn in range(len(arrived)):
        far = place_ref[0] ^ (turn + 1)
        for item in range(per_dev):
            pair = read_ref[far * per_dev + item]
            own = coef_ref[jnp.maximum(pair, 0)]
            out_ref[turn * per_dev + item] = dot(own, arrived[turn][item], 0, 0).astype(
                jnp.bfloat16
            )


def add_coupling(slots, all_slots, place_ref, read_ref, weight_ref, proj_ref, amps_ref, part_ref):
    per_dev = slots * MOST
    width = proj_ref.shape[-1]

    def body(turn, carry):
        far = place_ref[0] ^ (turn + 1)
        terms = []
        for item in range(per_dev):
            slot = place_ref[1] * slots + item // MOST
            pair = read_ref[(far * all_slots + slot) * MOST + item % MOST]
            safe = jnp.maximum(pair, 0)
            weight = jnp.where(pair >= 0, weight_ref[safe * all_slots + slot], 0.0)
            proj = proj_ref[turn * per_dev + item]
            amps = amps_ref[far, :, item].reshape(width, width)
            mixed = dot(proj, amps, 1, 0).astype(jnp.bfloat16)
            terms.append((safe, weight * dot(mixed, proj, 1, 1)))
        for safe, term in terms:
            part_ref[safe] += term
        return carry

    lax.fori_loop(0, proj_ref.shape[0] // per_dev, body, 0)


def coupling_kernel(
    slots, all_slots, scaled, place_ref, read_ref, weight_ref, proj_ref, amps_ref, start_ref,
    out_ref, own_ref, part_ref,
):
    part_ref[...] = jnp.zeros_like(part_ref)
    add_coupling(slots, all_slots, place_ref, read_ref, weight_ref, proj_ref, amps_ref, part_ref)
    pairs, rows, width = own_ref.shape
    parts = width // rows
    row_start = pl.multiple_of(place_ref[1] * rows, rows)

    if not scaled:

        def body(pair, carry):
            total = (part_ref[pair] + start_ref[pair]).astype(out_ref.dtype)
            for part in range(parts):
                out_ref[part, pair] = total[part * rows : (part + 1) * rows]
            at = pl.ds(row_start, rows)
            own_ref[pair] = part_ref[pair, at] + start_ref[pair, at]
            return carry

        lax.fori_loop(0, pairs, body, 0, unroll=2)
        return

    def body(pair, most):
        total = part_ref[pair] + start_ref[pair]
        for part in range(parts):
            piece = total[part * rows : (part + 1) * rows]
            out_ref[part, pair] = piece
            most = jnp.maximum(most, jnp.abs(piece))
        at = pl.ds(row_start, rows)
        own_ref[pair] = part_ref[pair, at] + start_ref[pair, at]
        return most

    most = lax.fori_loop(0, pairs, body, jnp.zeros((rows, width), jnp.float32), unroll=2)
    most = jnp.max(jnp.max(most, axis=0, keepdims=True), axis=1, keepdims=True)
    power = jnp.maximum(jnp.ceil(jnp.log2(jnp.maximum(most, 1.0)) - 15.0), 0.0)
    for part in range(parts):
        out_ref[part, pairs] = jnp.broadcast_to(power, (rows, width))


def first_update_kernel(
    send_ref, sum_ref, own_ref, scale_ref, kept_ref, new_ref, half_ref, out_ref
):
    def body(pair, carry):
        new = kept_ref[pair] - (sum_ref[pair] + own_ref[pair]) * scale_ref[pair]
        new_ref[pair] = new
        half_ref[pair] = new.astype(jnp.bfloat16)
        return carry

    lax.fori_loop(0, new_ref.shape[0], body, 0, unroll=4)
    pack_rows(send_ref, half_ref, out_ref)


def between_kernel(
    place_ref, energy_ref, fock_ref, kept_ref, half_ref, before_ref, sum_ref, old_ref,
    part_ref, own_ref,
):
    block, rows, width = kept_ref.shape
    first = pl.program_id(0) * block
    row_start = pl.multiple_of(place_ref[1] * rows, rows)
    for pair in range(block):
        half = half_ref[pair]
        fock_rows = fock_ref[pair, pl.ds(row_start, rows), :]
        part_ref[pair] = (
            left_part(fock_rows, half) - left_part(fock_rows, before_ref[pair]) - old_ref[pair]
        )
        own_ref[pair] = (
            dot(half, fock_ref[pair], 1, 0)
            - energy_ref[first + pair] * kept_ref[pair]
            + sum_ref[pair]
        )


def last_update_kernel(place_ref, got_ref, mine_ref, own_ref, scale_ref, kept_ref, new_ref):
    def body(pair, carry):
        total = mine_ref[pair]
        for turn in range(1, got_ref.shape[0]):
            part = lax.rem(place_ref[1] + turn, got_ref.shape[0])
            total = total + got_ref[part, pair].astype(jnp.float32)
        new_ref[pair] = kept_ref[pair] - (total + own_ref[pair]) * scale_ref[pair]
        return carry

    lax.fori_loop(0, new_ref.shape[0], body, 0, unroll=4)


def shape(dims, dtype):
    return jax.ShapeDtypeStruct(tuple(dims), dtype)


def per_device(
    pair_orbits,
    pno_count,
    partner,
    couple_orbit,
    couple_side,
    occ_fock,
    fit_left,
    fit_right,
    pno_coef,
    virt_fock,
    amps_in,
):
    pair_dev = pno_count.shape[0]
    width = virt_fock.shape[1]
    rows = amps_in.shape[1]
    slots = partner.shape[1]
    dev_count = lax.axis_size("pairs")
    aux_count = lax.axis_size("aux")
    all_slots = slots * aux_count
    per_dev = slots * MOST
    bf16, f32 = jnp.bfloat16, jnp.float32
    place = jnp.stack([lax.axis_index("pairs"), lax.axis_index("aux")]).astype(jnp.int32)

    coef_send, coef_read = pair_places(partner, pair_dev, dev_count)

    coef_out = pl.pallas_call(
        functools.partial(coef_kernel, slots),
        out_shape=tuple(
            shape((per_dev,) + pno_coef.shape[1:], bf16) for _ in range(dev_count - 1)
        ),
        in_specs=[SMEM, SMEM, ANY],
        out_specs=tuple(HBM for _ in range(dev_count - 1)),
        scratch_shapes=[
            pltpu.VMEM(((dev_count - 1) * per_dev,) + pno_coef.shape[1:], bf16),
            pltpu.SemaphoreType.DMA(((dev_count - 1) * per_dev,)),
            pltpu.SemaphoreType.DMA((dev_count - 1,)),
        ],
        compiler_params=params(),
        name="pack_coef",
    )(place, coef_send, pno_coef)

    tables = jnp.concatenate([partner, couple_orbit, couple_side], axis=1)
    tables, coef_out = lax.optimization_barrier((tables, coef_out))
    coef_far = [
        lax.ppermute(coef_out[turn], "pairs", [(dev, dev ^ (turn + 1)) for dev in range(dev_count)])
        for turn in range(dev_count - 1)
    ]

    shares = [tables] + [
        lax.ppermute(tables, "aux", [(dev, (dev + turn) % aux_count) for dev in range(aux_count)])
        for turn in range(1, aux_count)
    ]
    tables = jnp.zeros((aux_count,) + tables.shape, jnp.int32)
    owners = jnp.arange(aux_count)[:, None, None]
    for turn, share in enumerate(shares):
        owner = lax.rem(place[1] + aux_count - turn, aux_count)
        tables = jnp.where(owners == owner, share[None], tables)
    tables = tables.reshape(aux_count, pair_dev, 3, slots).transpose(2, 1, 0, 3)
    tables = tables.reshape(3, pair_dev, all_slots)
    partner, couple_orbit, couple_side = tables[0], tables[1], tables[2]
    send, read = pair_places(partner, pair_dev, dev_count)

    occ_ids = jnp.arange(occ_fock.shape[0], dtype=jnp.int32)
    occ_diag = jnp.diagonal(occ_fock)
    energy = jnp.sum(
        jnp.where(pair_orbits[:, :, None] == occ_ids[None, None, :], occ_diag[None, None, :], 0.0),
        axis=(1, 2),
    )
    free_orbit = jnp.where(couple_side == 0, pair_orbits[:, 0:1], pair_orbits[:, 1:2])
    onehot = (couple_orbit.reshape(-1)[:, None] == occ_ids[None, :]).astype(f32)
    fock_rows = jnp.dot(onehot, occ_fock, precision=precise)
    weight = -jnp.sum(
        jnp.where(free_orbit.reshape(-1)[:, None] == occ_ids[None, :], fock_rows, 0.0), axis=1
    )

    places = dev_count * all_slots * MOST
    kept, half, amps_out = pl.pallas_call(
        start_kernel,
        out_shape=(
            shape(amps_in.shape, f32),
            shape(amps_in.shape, bf16),
            shape((places, rows, width), bf16),
        ),
        in_specs=[SMEM, SMEM, SMEM, VMEM],
        out_specs=(VMEM, VMEM, VMEM),
        compiler_params=params(),
        name="mask_and_pack",
    )(place, send, pno_count, amps_in)

    def exchange(packed):
        packed = packed.reshape(dev_count * aux_count, per_dev, rows, width)
        got = lax.all_to_all(packed, ("pairs", "aux"), split_axis=0, concat_axis=0, tiled=True)
        return got.reshape(dev_count, aux_count, per_dev, rows, width)

    amps_far = exchange(amps_out)
    block = 8
    by_pair = lambda *dims: pl.BlockSpec((block,) + dims, lambda step: (step,) + (0,) * len(dims))
    fit = fit_left.shape[2]
    wide = by_pair(width, width)
    slab = by_pair(rows, width)
    start, scale, own = pl.pallas_call(
        prepare_kernel,
        grid=(pair_dev // block,),
        out_shape=(
            shape((pair_dev, width, width), f32),
            shape(amps_in.shape, f32),
            shape(amps_in.shape, f32),
        ),
        in_specs=[SMEM, SMEM, SMEM, by_pair(width, fit), by_pair(width, fit), wide, slab, slab],
        out_specs=(wide, slab, slab),
        compiler_params=params(),
        cost_estimate=pl.CostEstimate(
            flops=2 * pair_dev * width * width * (fit + 2 * rows),
            bytes_accessed=2 * fit_left.size * 2 + pair_dev * width * width * 12,
            transcendentals=0,
        ),
        name="integrals",
    )(place, pno_count, energy, fit_left, fit_right, virt_fock, kept, half)

    items = (dev_count - 1) * per_dev
    projectors = pl.pallas_call(
        functools.partial(projector_kernel, slots),
        out_shape=shape((items, width, width), bf16),
        in_specs=[SMEM, SMEM] + [VMEM] * dev_count,
        out_specs=VMEM,
        compiler_params=params(),
        name="projectors",
    )(place, coef_read, pno_coef, *coef_far)

    def coupled(amps_far, start, scaled):
        if scaled:
            out = shape((aux_count, pair_dev + 1, rows, width), f32)
        else:
            out = shape((aux_count, pair_dev, rows, width), bf16)
        return pl.pallas_call(
            functools.partial(coupling_kernel, slots, all_slots, scaled),
            out_shape=(out, shape(amps_in.shape, f32), shape((pair_dev, width, width), f32)),
            in_specs=[SMEM, SMEM, SMEM, VMEM, VMEM, VMEM],
            out_specs=(VMEM, VMEM, VMEM),
            compiler_params=params(),
            name="coupling",
        )(place, read, weight, projectors, amps_far, start)

    to_sum, mine, part = coupled(amps_far, start, True)
    is_value = (jnp.arange(pair_dev + 1) < pair_dev)[None, :, None, None]
    power = to_sum[:, pair_dev:]
    to_sum = jnp.where(is_value, to_sum * jnp.exp2(-power), to_sum).astype(jnp.float16)
    got = lax.all_to_all(to_sum, "aux", split_axis=0, concat_axis=0, tiled=True)
    got = got.astype(f32)
    foreign = (jnp.arange(aux_count) != place[1])[:, None, None, None]
    got = jnp.where(foreign, got[:, :pair_dev] * jnp.exp2(got[:, pair_dev:]), 0.0)
    sums = mine + jnp.sum(got, axis=0)

    before = half
    kept, half, amps_out = pl.pallas_call(
        first_update_kernel,
        out_shape=(
            shape(amps_in.shape, f32),
            shape(amps_in.shape, bf16),
            shape((places, rows, width), bf16),
        ),
        in_specs=[SMEM] + [VMEM] * 4,
        out_specs=(VMEM,) * 3,
        compiler_params=params(),
        name="first_update",
    )(send, sums, own, scale, kept)

    amps_far = exchange(amps_out)

    start, own = pl.pallas_call(
        between_kernel,
        grid=(pair_dev // block,),
        out_shape=(shape((pair_dev, width, width), f32), shape(amps_in.shape, f32)),
        in_specs=[SMEM, SMEM, wide, slab, slab, slab, slab, wide],
        out_specs=(wide, slab),
        compiler_params=params(),
        cost_estimate=pl.CostEstimate(
            flops=6 * pair_dev * width * width * rows,
            bytes_accessed=pair_dev * width * width * 10,
            transcendentals=0,
        ),
        name="between",
    )(place, energy, virt_fock, kept, half, before, sums, part)

    to_sum, mine, _ = coupled(amps_far, start, False)
    got = lax.all_to_all(to_sum, "aux", split_axis=0, concat_axis=0, tiled=True)

    return pl.pallas_call(
        last_update_kernel,
        out_shape=shape(amps_in.shape, f32),
        in_specs=[SMEM] + [VMEM] * 5,
        out_specs=VMEM,
        compiler_params=params(),
        name="last_update",
    )(place, got, mine, own, scale, kept)


def solution(mesh):
    return jax.shard_map(
        per_device,
        mesh=mesh,
        in_specs=(
            P("pairs", None),
            P("pairs"),
            P("pairs", "aux"),
            P("pairs", "aux"),
            P("pairs", "aux"),
            P(),
            P("pairs", None, "aux"),
            P("pairs", None, "aux"),
            P("pairs", None, None),
            P("pairs", None, None),
            P("pairs", "aux", None),
        ),
        out_specs=P("pairs", "aux", None),
        check_vma=False,
    )
```

```python
import functools

import jax
import jax.numpy as jnp
from jax import lax
from jax.experimental import pallas as pl
from jax.experimental.pallas import tpu as pltpu
from jax.sharding import PartitionSpec as P

MOST = 2
SPARE_BYTES = 3 * 1024 * 1024
WIDE_BYTES = 48 * 1024 * 1024

SMEM = pl.BlockSpec(memory_space=pltpu.SMEM)
VMEM = pl.BlockSpec(memory_space=pltpu.VMEM)
HBM = pl.BlockSpec(memory_space=pltpu.HBM)
FREE = pl.CostEstimate(flops=0, bytes_accessed=0, transcendentals=0)


def dot(left, right, over_left, over_right):
    return lax.dot_general(
        left, right, (((over_left,), (over_right,)), ((), ())), preferred_element_type=jnp.float32
    )


def params(*arrays):
    held = sum(array.size * array.dtype.itemsize for array in arrays)
    needed = held + held // 8 + SPARE_BYTES
    return pltpu.CompilerParams(vmem_limit_bytes=max(needed, WIDE_BYTES))


def pair_places(partner, pair_dev, dev_count, arrival):
    slots = partner.shape[1]
    owner = jnp.where(partner >= 0, partner // pair_dev, -1)
    own_id = jnp.broadcast_to(jnp.arange(pair_dev, dtype=jnp.int32)[:, None], partner.shape)
    far_key = (partner - owner * pair_dev) * pair_dev + own_id
    none = pair_dev * pair_dev
    devs = jnp.arange(dev_count, dtype=jnp.int32)[None, :, None]
    hit = owner[:, None, :] == devs

    def ranked(key):
        left = jnp.where(hit, key[:, None, :], none)
        found = []
        for _ in range(MOST):
            least = jnp.min(left, axis=0)
            found.append(least)
            left = jnp.where(left == least[None], none, left)
        return jnp.stack(found, axis=-1).reshape(-1)

    send = ranked(own_id)
    send = jnp.where(send < none, send, 0)
    if not arrival:
        return send
    read = ranked(far_key)
    return send, jnp.where(read < none, lax.rem(read, pair_dev), -1)


def pack_rows(send_ref, half_ref, out_ref, held, sems):
    chunk = held.shape[0] // sems.shape[0]

    def store(turn):
        at = pl.ds(pl.multiple_of(turn * chunk, chunk), chunk)
        return pltpu.make_async_copy(held.at[at], out_ref.at[at], sems.at[turn])

    def body(turn, carry):
        for item in range(chunk):
            place = turn * chunk + item
            held[place] = half_ref[send_ref[place]]
        store(turn).start()
        return carry

    def finish(turn, carry):
        store(turn).wait()
        return carry

    lax.fori_loop(0, sems.shape[0], body, 0)
    lax.fori_loop(0, sems.shape[0], finish, 0)


def start_kernel(
    place_ref, send_ref, count_ref, amps_ref, kept_ref, half_ref, out_ref, held, sems
):
    pairs, rows, width = amps_ref.shape
    row_id = lax.broadcasted_iota(jnp.int32, (rows, width), 0) + place_ref[1] * rows
    col_id = lax.broadcasted_iota(jnp.int32, (rows, width), 1)
    last = jnp.maximum(row_id, col_id)

    def body(pair, carry):
        kept = jnp.where(last < count_ref[pair], amps_ref[pair], 0.0)
        kept_ref[pair] = kept
        half_ref[pair] = kept.astype(jnp.bfloat16)
        return carry

    lax.fori_loop(0, pairs, body, 0, unroll=4)
    pack_rows(send_ref, half_ref, out_ref, held, sems)


def coef_kernel(slots, place_ref, send_ref, coef_ref, *rest):
    outs, (held, in_sems, out_sems) = rest[:-3], rest[-3:]
    per_dev = slots * MOST

    def fetch(turn, item):
        far = place_ref[0] ^ (turn + 1)
        pair = send_ref[far * per_dev + item]
        place = turn * per_dev + item
        return pltpu.make_async_copy(coef_ref.at[pair], held.at[place], in_sems.at[place])

    def store(turn):
        return pltpu.make_async_copy(
            held.at[pl.ds(turn * per_dev, per_dev)], outs[turn], out_sems.at[turn]
        )

    for turn in range(len(outs)):
        for item in range(per_dev):
            fetch(turn, item).start()
    for turn in range(len(outs)):
        for item in range(per_dev):
            fetch(turn, item).wait()
        store(turn).start()
    for turn in range(len(outs)):
        store(turn).wait()


def put_rows(out_ref, pair, value):
    rows = out_ref.shape[2]
    for part in range(out_ref.shape[0]):
        out_ref[part, pair] = value[part * rows : (part + 1) * rows]


def element(matrix_ref, row, column):
    line = matrix_ref[pl.ds(row, 1), :]
    at = lax.broadcasted_iota(jnp.int32, line.shape, 1) == column
    return jnp.sum(jnp.where(at, line, 0.0), axis=1, keepdims=True)


def left_part(fock_rows, half_rows):
    return dot(fock_rows, half_rows, 0, 0)


def prepare_kernel(
    place_ref, count_ref, orbit_ref, occ_ref, left_ref, right_ref, fock_ref, kept_ref, half_ref,
    part_ref, scale_ref, own_ref, energy_ref,
):
    block, rows, width = kept_ref.shape
    first = pl.program_id(0) * block
    row_start = pl.multiple_of(place_ref[1] * rows, rows)
    row_id = lax.broadcasted_iota(jnp.int32, (rows, width), 0) + row_start
    col_id = lax.broadcasted_iota(jnp.int32, (rows, width), 1)
    last = jnp.maximum(row_id, col_id)
    eye_rows = row_id == col_id
    eye = lax.broadcasted_iota(jnp.int32, (width, width), 0) == lax.broadcasted_iota(
        jnp.int32, (width, width), 1
    )
    for pair in range(block):
        at = orbit_ref.shape[0] - 2 * (count_ref.shape[0] - first - pair)
        orbit, other = orbit_ref[at], orbit_ref[at + 1]
        energy = element(occ_ref, orbit, orbit) + element(occ_ref, other, other)
        energy_ref[pair] = jnp.broadcast_to(energy, (1, width))
        fock = fock_ref[pair]
        fock_rows = fock_ref[pair, pl.ds(row_start, rows), :]
        half = half_ref[pair]
        fitted = dot(left_ref[pair], right_ref[pair], 1, 1)
        put_rows(part_ref, pair, fitted + left_part(fock_rows, half))
        own_ref[pair] = dot(half, fock, 1, 0) - energy * kept_ref[pair]
        diag_cols = jnp.sum(jnp.where(eye, fock.astype(jnp.float32), 0.0), axis=0, keepdims=True)
        diag_rows = jnp.sum(
            jnp.where(eye_rows, fock_rows.astype(jnp.float32), 0.0), axis=1, keepdims=True
        )
        denominator = diag_rows + diag_cols - energy
        scale_ref[pair] = jnp.where(last < count_ref[first + pair], 1.0 / denominator, 0.0)


def any_live(read_ref, first, per_dev, rank):
    most = read_ref[first + rank]
    for item in range(rank + MOST, per_dev, MOST):
        most = jnp.maximum(most, read_ref[first + item])
    return most >= 0


def own_coef_kernel(slots, place_ref, read_ref, coef_ref, out_ref):
    per_dev = slots * MOST

    def body(turn, carry):
        far = place_ref[0] ^ (turn + 1)
        for item in range(per_dev):
            pair = jnp.maximum(read_ref[far * per_dev + item], 0)
            out_ref[turn * per_dev + item] = coef_ref[pair].T
        return carry

    lax.fori_loop(0, out_ref.shape[0] // per_dev, body, 0)


def projector_kernel(turns, place_ref, read_ref, own_ref, *rest):
    arrived, out_ref = rest[:-1], rest[-1]
    per_dev = arrived[0].shape[0]

    def rank_items(place, turn, rank):
        for item in range(rank, per_dev, MOST):
            own = own_ref[turn * per_dev + item]
            out_ref[place * per_dev + item] = dot(own, arrived[place][item], 1, 0).astype(
                jnp.bfloat16
            )

    for place, turn in enumerate(turns):
        far = place_ref[0] ^ (turn + 1)
        for rank in range(MOST):
            pl.when(any_live(read_ref, far * per_dev, per_dev, rank))(
                functools.partial(rank_items, place, turn, rank)
            )


def add_coupling(
    groups, place_ref, read_ref, orbit_ref, occ_ref, proj_refs, fetch, amps_ref, part_ref
):
    per_dev = amps_ref.shape[2]
    slots = per_dev // MOST
    parts, pairs, rows = part_ref.shape[0], orbit_ref.shape[0] // (2 * slots + 2), part_ref.shape[2]
    side_at, pair_at = pairs * slots, 2 * pairs * slots

    def body(turn, place, proj_ref):
        width = proj_ref.shape[-1]
        far = place_ref[0] ^ (turn + 1)
        fetch(turn).wait()

        def rank_terms(rank):
            terms = []
            for item in range(rank, per_dev, MOST):
                pair = read_ref[far * per_dev + item]
                safe = jnp.maximum(pair, 0)
                entry = safe * slots + item // MOST
                orbit = orbit_ref[pair_at + 2 * safe + orbit_ref[side_at + entry]]
                coupled = element(occ_ref, orbit_ref[entry], orbit)
                weight = jnp.where(pair >= 0, -coupled, 0.0)
                proj = proj_ref[place * per_dev + item]
                amps = amps_ref[far, :, item].reshape(width, width)
                mixed = dot(proj, amps, 1, 0).astype(jnp.bfloat16)
                terms.append((safe, weight * dot(mixed, proj, 1, 1)))
            for safe, term in terms:
                for part in range(parts):
                    part_ref[part, safe] += term[part * rows : (part + 1) * rows]

        for rank in range(MOST):
            pl.when(any_live(read_ref, far * per_dev, per_dev, rank))(
                functools.partial(rank_terms, rank)
            )

    for turns, proj_ref in zip(groups, proj_refs):
        def step(place, carry, turns=turns, proj_ref=proj_ref):
            later = turns[min(1, len(turns) - 1)] - min(1, len(turns) - 1)
            body(jnp.where(place == 0, turns[0], place + later), place, proj_ref)
            return carry

        lax.fori_loop(0, len(turns), step, 0)


def coupling_kernel(
    groups, scaled, place_ref, read_ref, orbit_ref, occ_ref, early_ref, late_ref, amps_hbm,
    start_hbm, out_ref, extra_ref, amps_ref, amps_sems, start_sem, *rest,
):
    part_ref = out_ref if scaled else rest[0]
    parts, pairs, rows, width = start_hbm.shape

    def fetch(turn):
        far = place_ref[0] ^ (turn + 1)
        return pltpu.make_async_copy(amps_hbm.at[far], amps_ref.at[far], amps_sems.at[turn])

    loads = [
        pltpu.make_async_copy(
            start_hbm.at[part], part_ref.at[part, pl.ds(0, pairs)], start_sem.at[part]
        )
        for part in range(parts)
    ]
    for load in loads:
        load.start()
    for turns in groups:
        for turn in turns:
            fetch(turn).start()
    for load in loads:
        load.wait()
    add_coupling(
        groups, place_ref, read_ref, orbit_ref, occ_ref, (early_ref, late_ref), fetch, amps_ref,
        part_ref,
    )
    if not scaled:

        def body(pair, carry):
            for part in range(parts):
                out_ref[part, pair] = part_ref[part, pair].astype(out_ref.dtype)
            extra_ref[pair] = part_ref[place_ref[1], pair]
            return carry

        lax.fori_loop(0, pairs, body, 0, unroll=4)
        return

    def body(pair, most):
        for part in range(parts):
            most = jnp.maximum(most, jnp.abs(part_ref[part, pair]))
        return most

    most = lax.fori_loop(0, pairs, body, jnp.zeros((rows, width), jnp.float32), unroll=4)
    most = jnp.max(jnp.max(most, axis=0, keepdims=True), axis=1, keepdims=True)
    power = jnp.maximum(jnp.ceil(jnp.log2(jnp.maximum(most, 1.0)) - 15.0), 0.0)
    for part in range(parts):
        out_ref[part, pairs] = jnp.broadcast_to(power * jnp.exp2(power), (rows, width))
    extra_ref[...] = jnp.broadcast_to(jnp.exp2(-power), (1, width))


def first_update_kernel(
    send_ref, sum_ref, own_ref, scale_ref, kept_ref, new_ref, half_ref, out_ref, held, sems
):
    def body(pair, carry):
        new = kept_ref[pair] - (sum_ref[pair] + own_ref[pair]) * scale_ref[pair]
        new_ref[pair] = new
        half_ref[pair] = new.astype(jnp.bfloat16)
        return carry

    lax.fori_loop(0, new_ref.shape[0], body, 0, unroll=4)
    pack_rows(send_ref, half_ref, out_ref, held, sems)


def between_kernel(
    place_ref, energy_ref, fock_ref, kept_ref, half_ref, before_ref, sum_ref, start_ref, old_ref,
    part_ref, own_ref,
):
    block, rows, width = kept_ref.shape
    row_start = pl.multiple_of(place_ref[1] * rows, rows)
    for pair in range(block):
        half = half_ref[pair]
        fock_rows = fock_ref[pair, pl.ds(row_start, rows), :]
        change = left_part(fock_rows, half) - left_part(fock_rows, before_ref[pair])
        for part in range(part_ref.shape[0]):
            part_ref[part, pair] = (
                start_ref[part, pair] - old_ref[part, pair] + change[part * rows : (part + 1) * rows]
            )
        own_ref[pair] = (
            dot(half, fock_ref[pair], 1, 0)
            - energy_ref[pair] * kept_ref[pair]
            + sum_ref[pair]
        )


def last_update_kernel(place_ref, got_ref, mine_ref, own_ref, scale_ref, kept_ref, new_ref):
    def body(pair, carry):
        total = mine_ref[pair]
        for turn in range(1, got_ref.shape[0]):
            part = lax.rem(place_ref[1] + turn, got_ref.shape[0])
            total = total + got_ref[part, pair].astype(jnp.float32)
        new_ref[pair] = kept_ref[pair] - (total + own_ref[pair]) * scale_ref[pair]
        return carry

    lax.fori_loop(0, new_ref.shape[0], body, 0, unroll=4)


def shape(dims, dtype):
    return jax.ShapeDtypeStruct(tuple(dims), dtype)


def per_device(
    pair_orbits,
    pno_count,
    partner,
    couple_orbit,
    couple_side,
    occ_fock,
    fit_left,
    fit_right,
    pno_coef,
    virt_fock,
    amps_in,
):
    pair_dev = pno_count.shape[0]
    width = virt_fock.shape[1]
    rows = amps_in.shape[1]
    slots = partner.shape[1]
    dev_count = lax.axis_size("pairs")
    aux_count = lax.axis_size("aux")
    all_slots = slots * aux_count
    per_dev = slots * MOST
    items = (dev_count - 1) * per_dev
    bf16, f32 = jnp.bfloat16, jnp.float32
    place = jnp.stack([lax.axis_index("pairs"), lax.axis_index("aux")]).astype(jnp.int32)

    orbits = [couple_orbit.reshape(-1), couple_side.reshape(-1), pair_orbits.reshape(-1)]
    orbits = jnp.concatenate(orbits)
    coef_send, coef_read = pair_places(partner, pair_dev, dev_count, True)

    coef_out = pl.pallas_call(
        functools.partial(coef_kernel, slots),
        out_shape=tuple(
            shape((per_dev,) + pno_coef.shape[1:], bf16) for _ in range(dev_count - 1)
        ),
        in_specs=[SMEM, SMEM, HBM],
        out_specs=tuple(HBM for _ in range(dev_count - 1)),
        scratch_shapes=[
            pltpu.VMEM(((dev_count - 1) * per_dev,) + pno_coef.shape[1:], bf16),
            pltpu.SemaphoreType.DMA(((dev_count - 1) * per_dev,)),
            pltpu.SemaphoreType.DMA((dev_count - 1,)),
        ],
        compiler_params=params(shape((items,) + pno_coef.shape[1:], bf16)),
        cost_estimate=FREE,
        name="pack_coef",
    )(place, coef_send, pno_coef)

    tables = partner
    tables, coef_out = lax.optimization_barrier((tables, coef_out))
    coef_far = [
        lax.ppermute(coef_out[turn], "pairs", [(dev, dev ^ (turn + 1)) for dev in range(dev_count)])
        for turn in range(dev_count - 1)
    ]

    shares = [tables] + [
        lax.ppermute(tables, "aux", [(dev, (dev + turn) % aux_count) for dev in range(aux_count)])
        for turn in range(1, aux_count)
    ]
    tables = jnp.zeros((aux_count,) + tables.shape, jnp.int32)
    owners = jnp.arange(aux_count)[:, None, None]
    for turn, share in enumerate(shares):
        owner = lax.rem(place[1] + aux_count - turn, aux_count)
        tables = jnp.where(owners == owner, share[None], tables)
    tables = tables.transpose(1, 0, 2).reshape(pair_dev, all_slots)
    send = pair_places(tables, pair_dev, dev_count, False)

    places = dev_count * all_slots * MOST
    packed = shape((places, rows, width), bf16)
    pack_scratch = [pltpu.VMEM(packed.shape, bf16), pltpu.SemaphoreType.DMA((dev_count,))]
    kept, half, amps_out = pl.pallas_call(
        start_kernel,
        out_shape=(
            shape(amps_in.shape, f32),
            shape(amps_in.shape, bf16),
            packed,
        ),
        in_specs=[SMEM, SMEM, SMEM, VMEM],
        out_specs=(VMEM, VMEM, HBM),
        scratch_shapes=pack_scratch,
        compiler_params=params(amps_in, amps_in, amps_in, packed),
        cost_estimate=FREE,
        name="mask_and_pack",
    )(place, send, pno_count, amps_in)

    def exchange(packed):
        packed = packed.reshape(dev_count * aux_count, per_dev, rows, width)
        got = lax.all_to_all(packed, ("pairs", "aux"), split_axis=0, concat_axis=0, tiled=True)
        return got.reshape(dev_count, aux_count, per_dev, rows, width)

    ahead = slice(1, dev_count // 2 + 1)
    amps_out, coef_far[ahead] = lax.optimization_barrier((amps_out, coef_far[ahead]))
    amps_far = exchange(amps_out)

    block = 8
    by_pair = lambda *dims: pl.BlockSpec((block,) + dims, lambda step: (step,) + (0,) * len(dims))
    fit = fit_left.shape[2]
    wide = by_pair(width, width)
    slab = by_pair(rows, width)
    line = by_pair(1, width)
    tall = pl.BlockSpec((aux_count, block, rows, width), lambda step: (0, step, 0, 0))
    by_rows = shape((aux_count, pair_dev, rows, width), f32)
    start, scale, own, energy = pl.pallas_call(
        prepare_kernel,
        grid=(pair_dev // block,),
        out_shape=(
            by_rows,
            shape(amps_in.shape, f32),
            shape(amps_in.shape, f32),
            shape((pair_dev, 1, width), f32),
        ),
        in_specs=[SMEM, SMEM, SMEM, VMEM, by_pair(width, fit), by_pair(width, fit), wide, slab, slab],
        out_specs=(tall, slab, slab, line),
        compiler_params=pltpu.CompilerParams(vmem_limit_bytes=WIDE_BYTES),
        cost_estimate=FREE,
        name="integrals",
    )(place, pno_count, orbits, occ_fock, fit_left, fit_right, virt_fock, kept, half)

    own_shape = shape((items, width, pno_coef.shape[1]), bf16)
    own_coef = pl.pallas_call(
        functools.partial(own_coef_kernel, slots),
        out_shape=own_shape,
        in_specs=[SMEM, SMEM, VMEM],
        out_specs=VMEM,
        compiler_params=params(pno_coef, own_shape),
        name="own_coef",
    )(place, coef_read, pno_coef)

    early = tuple(range(dev_count - 1)[ahead])
    groups = (early, tuple(turn for turn in range(dev_count - 1) if turn not in early))
    projectors = []
    for turns in groups:
        arrived = [coef_far[turn] for turn in turns]
        out = shape((len(turns) * per_dev, width, width), bf16)
        projectors.append(
            pl.pallas_call(
                functools.partial(projector_kernel, turns),
                out_shape=out,
                in_specs=[SMEM, SMEM] + [VMEM] * (1 + len(turns)),
                out_specs=VMEM,
                compiler_params=params(own_coef, out, *arrived),
                name="projectors",
            )(place, coef_read, own_coef, *arrived)
        )

    def coupled(amps_far, start, scaled):
        if scaled:
            out, extra = shape((aux_count, pair_dev + 1, rows, width), f32), shape((1, width), f32)
        else:
            out, extra = shape(start.shape, bf16), shape(amps_in.shape, f32)
        return pl.pallas_call(
            functools.partial(coupling_kernel, groups, scaled),
            out_shape=(out, extra),
            in_specs=[SMEM] * 3 + [VMEM] * 3 + [HBM] * 2,
            out_specs=(VMEM, VMEM),
            scratch_shapes=[
                pltpu.VMEM(amps_far.shape, bf16),
                pltpu.SemaphoreType.DMA((dev_count - 1,)),
                pltpu.SemaphoreType.DMA((aux_count,)),
            ]
            + ([] if scaled else [pltpu.VMEM(start.shape, f32)]),
            compiler_params=params(out, amps_in, start, amps_far, *projectors),
            name="coupling",
        )(place, coef_read, orbits, occ_fock, *projectors, amps_far, start)

    total, shrink = coupled(amps_far, start, True)
    to_sum = (total * shrink).astype(jnp.float16)
    got = lax.all_to_all(to_sum, "aux", split_axis=0, concat_axis=0, tiled=True)
    foreign = (jnp.arange(aux_count) != place[1])[:, None, None, None]
    grow = jnp.where(foreign, jnp.exp2(got[:, pair_dev:, :1].astype(f32)), 0.0)
    sums = lax.dynamic_index_in_dim(total, place[1], 0, keepdims=False)[:pair_dev]
    for turn in range(aux_count):
        sums = sums + got[turn, :pair_dev].astype(f32) * grow[turn]

    before = half
    kept, half, amps_out = pl.pallas_call(
        first_update_kernel,
        out_shape=(
            shape(amps_in.shape, f32),
            shape(amps_in.shape, bf16),
            packed,
        ),
        in_specs=[SMEM] + [VMEM] * 4,
        out_specs=(VMEM, VMEM, HBM),
        scratch_shapes=pack_scratch,
        compiler_params=params(amps_in, amps_in, amps_in, amps_in, amps_in, amps_in, packed),
        name="first_update",
    )(send, sums, own, scale, kept)

    amps_far = exchange(amps_out)

    start, own = pl.pallas_call(
        between_kernel,
        grid=(pair_dev // block,),
        out_shape=(by_rows, shape(amps_in.shape, f32)),
        in_specs=[SMEM, line, wide, slab, slab, slab, slab, tall, tall],
        out_specs=(tall, slab),
        compiler_params=params(*[shape((2 * block,) + dims, f32) for dims in ((width, 3 * width), (rows, 6 * width))]),
        cost_estimate=pl.CostEstimate(
            flops=6 * pair_dev * width * width * rows,
            bytes_accessed=pair_dev * width * width * 10,
            transcendentals=0,
        ),
        name="between",
    )(place, energy, virt_fock, kept, half, before, sums, start, total)

    to_sum, mine = coupled(amps_far, start, False)
    got = lax.all_to_all(to_sum, "aux", split_axis=0, concat_axis=0, tiled=True)

    return pl.pallas_call(
        last_update_kernel,
        out_shape=shape(amps_in.shape, f32),
        in_specs=[SMEM] + [VMEM] * 5,
        out_specs=VMEM,
        compiler_params=params(got, mine, own, scale, kept, amps_in),
        name="last_update",
    )(place, got, mine, own, scale, kept)


def solution(mesh):
    return jax.shard_map(
        per_device,
        mesh=mesh,
        in_specs=(
            P("pairs", None),
            P("pairs"),
            P("pairs", "aux"),
            P("pairs", "aux"),
            P("pairs", "aux"),
            P(),
            P("pairs", None, "aux"),
            P("pairs", None, "aux"),
            P("pairs", None, None),
            P("pairs", None, None),
            P("pairs", "aux", None),
        ),
        out_specs=P("pairs", "aux", None),
        check_vma=False,
    )
```

```python
import functools

import jax
import jax.numpy as jnp
from jax import lax
from jax.experimental import pallas as pl
from jax.experimental.pallas import tpu as pltpu
from jax.sharding import PartitionSpec as P

MOST = 2
SPARE_BYTES = 3 * 1024 * 1024
WIDE_BYTES = 48 * 1024 * 1024

SMEM = pl.BlockSpec(memory_space=pltpu.SMEM)
VMEM = pl.BlockSpec(memory_space=pltpu.VMEM)
HBM = pl.BlockSpec(memory_space=pltpu.HBM)
FREE = pl.CostEstimate(flops=0, bytes_accessed=0, transcendentals=0)


def dot(left, right, over_left, over_right):
    return lax.dot_general(
        left, right, (((over_left,), (over_right,)), ((), ())), preferred_element_type=jnp.float32
    )


def params(*arrays):
    held = sum(array.size * array.dtype.itemsize for array in arrays)
    needed = held + held // 8 + SPARE_BYTES
    return pltpu.CompilerParams(vmem_limit_bytes=max(needed, WIDE_BYTES))


def pair_places(partner, pair_dev, dev_count, arrival):
    slots = partner.shape[1]
    owner = jnp.where(partner >= 0, partner // pair_dev, -1)
    own_id = jnp.broadcast_to(jnp.arange(pair_dev, dtype=jnp.int32)[:, None], partner.shape)
    far_key = (partner - owner * pair_dev) * pair_dev + own_id
    none = pair_dev * pair_dev
    devs = jnp.arange(dev_count, dtype=jnp.int32)[None, :, None]
    hit = owner[:, None, :] == devs

    def ranked(key):
        left = jnp.where(hit, key[:, None, :], none)
        found = []
        for _ in range(MOST):
            least = jnp.min(left, axis=0)
            found.append(least)
            left = jnp.where(left == least[None], none, left)
        return jnp.stack(found, axis=-1).reshape(-1)

    send = ranked(own_id)
    send = jnp.where(send < none, send, 0)
    if not arrival:
        return send
    read = ranked(far_key)
    return send, jnp.where(read < none, lax.rem(read, pair_dev), -1)


def pack_rows(send_ref, half_ref, out_ref, held, sems):
    chunk = held.shape[0] // sems.shape[0]

    def store(turn):
        at = pl.ds(pl.multiple_of(turn * chunk, chunk), chunk)
        return pltpu.make_async_copy(held.at[at], out_ref.at[at], sems.at[turn])

    def body(turn, carry):
        for item in range(chunk):
            place = turn * chunk + item
            held[place] = half_ref[send_ref[place]]
        store(turn).start()
        return carry

    def finish(turn, carry):
        store(turn).wait()
        return carry

    lax.fori_loop(0, sems.shape[0], body, 0)
    lax.fori_loop(0, sems.shape[0], finish, 0)


def start_kernel(
    place_ref, send_ref, count_ref, amps_ref, kept_ref, half_ref, out_ref, held, sems
):
    pairs, rows, width = amps_ref.shape
    row_id = lax.broadcasted_iota(jnp.int32, (rows, width), 0) + place_ref[1] * rows
    col_id = lax.broadcasted_iota(jnp.int32, (rows, width), 1)
    last = jnp.maximum(row_id, col_id)

    def body(pair, carry):
        kept = jnp.where(last < count_ref[pair], amps_ref[pair], 0.0)
        kept_ref[pair] = kept
        half_ref[pair] = kept.astype(jnp.bfloat16)
        return carry

    lax.fori_loop(0, pairs, body, 0, unroll=4)
    pack_rows(send_ref, half_ref, out_ref, held, sems)


def coef_kernel(slots, place_ref, send_ref, coef_ref, *rest):
    outs, (held, in_sems, out_sems) = rest[:-3], rest[-3:]
    per_dev = slots * MOST

    def fetch(turn, item):
        far = place_ref[0] ^ (turn + 1)
        pair = send_ref[far * per_dev + item]
        place = turn * per_dev + item
        return pltpu.make_async_copy(coef_ref.at[pair], held.at[place], in_sems.at[place])

    def store(turn):
        return pltpu.make_async_copy(
            held.at[pl.ds(turn * per_dev, per_dev)], outs[turn], out_sems.at[turn]
        )

    for turn in range(len(outs)):
        for item in range(per_dev):
            fetch(turn, item).start()
    for turn in range(len(outs)):
        for item in range(per_dev):
            fetch(turn, item).wait()
        store(turn).start()
    for turn in range(len(outs)):
        store(turn).wait()


def put_rows(out_ref, pair, value):
    rows = out_ref.shape[2]
    for part in range(out_ref.shape[0]):
        out_ref[part, pair] = value[part * rows : (part + 1) * rows]


def element(matrix_ref, row, column):
    line = matrix_ref[pl.ds(row, 1), :]
    at = lax.broadcasted_iota(jnp.int32, line.shape, 1) == column
    return jnp.sum(jnp.where(at, line, 0.0), axis=1, keepdims=True)


def left_part(fock_rows, half_rows):
    return dot(fock_rows, half_rows, 0, 0)


def prepare_kernel(
    place_ref, count_ref, orbit_ref, occ_ref, left_ref, right_ref, fock_ref, kept_ref, half_ref,
    part_ref, scale_ref, own_ref, energy_ref,
):
    block, rows, width = kept_ref.shape
    first = pl.program_id(0) * block
    row_start = pl.multiple_of(place_ref[1] * rows, rows)
    row_id = lax.broadcasted_iota(jnp.int32, (rows, width), 0) + row_start
    col_id = lax.broadcasted_iota(jnp.int32, (rows, width), 1)
    last = jnp.maximum(row_id, col_id)
    eye_rows = row_id == col_id
    eye = lax.broadcasted_iota(jnp.int32, (width, width), 0) == lax.broadcasted_iota(
        jnp.int32, (width, width), 1
    )
    for pair in range(block):
        at = orbit_ref.shape[0] - 2 * (count_ref.shape[0] - first - pair)
        orbit, other = orbit_ref[at], orbit_ref[at + 1]
        energy = element(occ_ref, orbit, orbit) + element(occ_ref, other, other)
        energy_ref[pair] = jnp.broadcast_to(energy, (1, width))
        fock = fock_ref[pair]
        fock_rows = fock_ref[pair, pl.ds(row_start, rows), :]
        half = half_ref[pair]
        fitted = dot(left_ref[pair], right_ref[pair], 1, 1)
        put_rows(part_ref, pair, fitted + left_part(fock_rows, half))
        own_ref[pair] = dot(half, fock, 1, 0) - energy * kept_ref[pair]
        diag_cols = jnp.sum(jnp.where(eye, fock.astype(jnp.float32), 0.0), axis=0, keepdims=True)
        diag_rows = jnp.sum(
            jnp.where(eye_rows, fock_rows.astype(jnp.float32), 0.0), axis=1, keepdims=True
        )
        denominator = diag_rows + diag_cols - energy
        scale_ref[pair] = jnp.where(last < count_ref[first + pair], 1.0 / denominator, 0.0)


def any_live(read_ref, first, per_dev, rank):
    most = read_ref[first + rank]
    for item in range(rank + MOST, per_dev, MOST):
        most = jnp.maximum(most, read_ref[first + item])
    return most >= 0


def own_coef_kernel(slots, place_ref, read_ref, coef_ref, out_ref):
    per_dev = slots * MOST

    def body(turn, carry):
        far = place_ref[0] ^ (turn + 1)
        for item in range(per_dev):
            pair = jnp.maximum(read_ref[far * per_dev + item], 0)
            out_ref[turn * per_dev + item] = coef_ref[pair].T
        return carry

    lax.fori_loop(0, out_ref.shape[0] // per_dev, body, 0)


def projector_kernel(turns, place_ref, read_ref, own_ref, *rest):
    arrived, out_ref = rest[:-1], rest[-1]
    per_dev = arrived[0].shape[0]

    def rank_items(place, turn, rank):
        for item in range(rank, per_dev, MOST):
            own = own_ref[turn * per_dev + item]
            out_ref[place * per_dev + item] = dot(own, arrived[place][item], 1, 0).astype(
                jnp.bfloat16
            )

    for place, turn in enumerate(turns):
        far = place_ref[0] ^ (turn + 1)
        for rank in range(MOST):
            pl.when(any_live(read_ref, far * per_dev, per_dev, rank))(
                functools.partial(rank_items, place, turn, rank)
            )


def add_coupling(sets, place_ref, occ_ref, fetch, amps_ref, part_ref):
    parts, rows, width = part_ref.shape[0], part_ref.shape[2], part_ref.shape[3]
    per_dev = amps_ref.shape[2] // len(sets)
    slots = per_dev // MOST
    pairs = sets[0][1].shape[0] // (2 * slots + 2)
    side_at, pair_at = pairs * slots, 2 * pairs * slots

    def body(turn, place, proj_ref, read_ref, orbit_ref, offset):
        far = place_ref[0] ^ (turn + 1)
        if offset == 0:
            fetch(turn).wait()

        def rank_terms(rank):
            terms = []
            for item in range(rank, per_dev, MOST):
                pair = read_ref[far * per_dev + item]
                safe = jnp.maximum(pair, 0)
                entry = safe * slots + item // MOST
                orbit = orbit_ref[pair_at + 2 * safe + orbit_ref[side_at + entry]]
                coupled = element(occ_ref, orbit_ref[entry], orbit)
                weight = jnp.where(pair >= 0, -coupled, 0.0)
                proj = proj_ref[place * per_dev + item]
                amps = amps_ref[far, :, offset + item].reshape(width, width)
                mixed = dot(proj, amps, 1, 0).astype(jnp.bfloat16)
                terms.append((safe, weight * dot(mixed, proj, 1, 1)))
            for safe, term in terms:
                for part in range(parts):
                    part_ref[part, safe] += term[part * rows : (part + 1) * rows]

        for rank in range(MOST):
            pl.when(any_live(read_ref, far * per_dev, per_dev, rank))(
                functools.partial(rank_terms, rank)
            )

    for number, (read_ref, orbit_ref, groups) in enumerate(sets):
        for turns, proj_ref in groups:
            later = turns[min(1, len(turns) - 1)] - min(1, len(turns) - 1)

            def step(place, carry, first=turns[0], later=later, proj_ref=proj_ref):
                turn = jnp.where(place == 0, first, place + later)
                body(turn, place, proj_ref, read_ref, orbit_ref, number * per_dev)
                return carry

            lax.fori_loop(0, len(turns), step, 0)


def coupling_kernel(groups, scaled, place_ref, *refs):
    set_count = 1 if scaled else 2
    tables, refs = refs[: 2 * set_count], refs[2 * set_count :]
    occ_ref, early_ref, late_ref = refs[:3]
    sets = [(tables[0], tables[1], list(zip(groups, (early_ref, late_ref))))]
    if not scaled:
        every = tuple(range(sum(len(turns) for turns in groups)))
        sets.append((tables[2], tables[3], [(every, refs[3])]))
    amps_hbm, start_hbm, out_ref, extra_ref, amps_ref, amps_sems, start_sem, *rest = refs[
        2 + set_count :
    ]
    part_ref = out_ref if scaled else rest[0]
    parts, pairs, rows, width = start_hbm.shape
    given = amps_hbm.shape[1]
    first_row = (place_ref[1] // given) * given

    def fetch(turn):
        far = place_ref[0] ^ (turn + 1)
        return pltpu.make_async_copy(
            amps_hbm.at[far], amps_ref.at[far, pl.ds(first_row, given)], amps_sems.at[turn]
        )

    loads = [
        pltpu.make_async_copy(
            start_hbm.at[part], part_ref.at[part, pl.ds(0, pairs)], start_sem.at[part]
        )
        for part in range(parts)
    ]
    for load in loads:
        load.start()
    for turns in groups:
        for turn in turns:
            fetch(turn).start()
    if given < parts:
        blank = jnp.zeros(amps_ref.shape[2:], amps_ref.dtype)

        def clear(far, carry):
            for row in range(parts - given):
                amps_ref[far, lax.rem(first_row + given + row, parts)] = blank
            return carry

        lax.fori_loop(0, amps_ref.shape[0], clear, 0)
    for load in loads:
        load.wait()
    add_coupling(sets, place_ref, occ_ref, fetch, amps_ref, part_ref)
    if not scaled:

        def body(pair, carry):
            for part in range(parts):
                out_ref[part, pair] = part_ref[part, pair].astype(out_ref.dtype)
            extra_ref[pair] = part_ref[place_ref[1], pair]
            return carry

        lax.fori_loop(0, pairs, body, 0, unroll=4)
        return

    def body(pair, most):
        for part in range(parts):
            most = jnp.maximum(most, jnp.abs(part_ref[part, pair]))
        return most

    most = lax.fori_loop(0, pairs, body, jnp.zeros((rows, width), jnp.float32), unroll=4)
    most = jnp.max(jnp.max(most, axis=0, keepdims=True), axis=1, keepdims=True)
    power = jnp.maximum(jnp.ceil(jnp.log2(jnp.maximum(most, 1.0)) - 15.0), 0.0)
    for part in range(parts):
        out_ref[part, pairs] = jnp.broadcast_to(power * jnp.exp2(power), (rows, width))
    extra_ref[...] = jnp.broadcast_to(jnp.exp2(-power), (1, width))


def first_update_kernel(
    send_ref, sum_ref, own_ref, scale_ref, kept_ref, new_ref, half_ref, out_ref, held, sems
):
    def body(pair, carry):
        new = kept_ref[pair] - (sum_ref[pair] + own_ref[pair]) * scale_ref[pair]
        new_ref[pair] = new
        half_ref[pair] = new.astype(jnp.bfloat16)
        return carry

    lax.fori_loop(0, new_ref.shape[0], body, 0, unroll=4)
    pack_rows(send_ref, half_ref, out_ref, held, sems)


def between_kernel(
    place_ref, energy_ref, fock_ref, kept_ref, half_ref, before_ref, sum_ref, start_ref, old_ref,
    part_ref, own_ref,
):
    block, rows, width = kept_ref.shape
    row_start = pl.multiple_of(place_ref[1] * rows, rows)
    for pair in range(block):
        half = half_ref[pair]
        fock_rows = fock_ref[pair, pl.ds(row_start, rows), :]
        change = left_part(fock_rows, half) - left_part(fock_rows, before_ref[pair])
        for part in range(part_ref.shape[0]):
            part_ref[part, pair] = (
                start_ref[part, pair] - old_ref[part, pair] + change[part * rows : (part + 1) * rows]
            )
        own_ref[pair] = (
            dot(half, fock_ref[pair], 1, 0)
            - energy_ref[pair] * kept_ref[pair]
            + sum_ref[pair]
        )


def last_update_kernel(place_ref, got_ref, mine_ref, own_ref, scale_ref, kept_ref, new_ref):
    def body(pair, carry):
        total = mine_ref[pair]
        for turn in range(1, got_ref.shape[0]):
            part = lax.rem(place_ref[1] + turn, got_ref.shape[0])
            total = total + got_ref[part, pair].astype(jnp.float32)
        new_ref[pair] = kept_ref[pair] - (total + own_ref[pair]) * scale_ref[pair]
        return carry

    lax.fori_loop(0, new_ref.shape[0], body, 0, unroll=4)


def shape(dims, dtype):
    return jax.ShapeDtypeStruct(tuple(dims), dtype)


def per_device(
    pair_orbits,
    pno_count,
    partner,
    couple_orbit,
    couple_side,
    occ_fock,
    fit_left,
    fit_right,
    pno_coef,
    virt_fock,
    amps_in,
):
    pair_dev = pno_count.shape[0]
    width = virt_fock.shape[1]
    rows = amps_in.shape[1]
    slots = partner.shape[1]
    dev_count = lax.axis_size("pairs")
    aux_count = lax.axis_size("aux")
    all_slots = slots * aux_count
    per_dev = slots * MOST
    items = (dev_count - 1) * per_dev
    bf16, f32 = jnp.bfloat16, jnp.float32
    place = jnp.stack([lax.axis_index("pairs"), lax.axis_index("aux")]).astype(jnp.int32)

    orbits = [couple_orbit.reshape(-1), couple_side.reshape(-1), pair_orbits.reshape(-1)]
    orbits = jnp.concatenate(orbits)
    coef_send, coef_read = pair_places(partner, pair_dev, dev_count, True)

    def packed_coef(send):
        return pl.pallas_call(
            functools.partial(coef_kernel, slots),
            out_shape=tuple(
                shape((per_dev,) + pno_coef.shape[1:], bf16) for _ in range(dev_count - 1)
            ),
            in_specs=[SMEM, SMEM, HBM],
            out_specs=tuple(HBM for _ in range(dev_count - 1)),
            scratch_shapes=[
                pltpu.VMEM((items,) + pno_coef.shape[1:], bf16),
                pltpu.SemaphoreType.DMA((items,)),
                pltpu.SemaphoreType.DMA((dev_count - 1,)),
            ],
            compiler_params=params(shape((items,) + pno_coef.shape[1:], bf16)),
            cost_estimate=FREE,
            name="pack_coef",
        )(place, send, pno_coef)

    def sent_coef(coef_out):
        return [
            lax.ppermute(packed, "pairs", [(dev, dev ^ (turn + 1)) for dev in range(dev_count)])
            for turn, packed in enumerate(coef_out)
        ]

    coef_out = packed_coef(coef_send)
    tables = partner
    tables, coef_out = lax.optimization_barrier((tables, coef_out))
    coef_far = sent_coef(coef_out)
    half_count = aux_count // 2
    more = jnp.concatenate([tables, couple_orbit, couple_side], axis=1)
    shares = [tables]
    for turn in range(1, aux_count):
        turned = [(dev, (dev + turn) % aux_count) for dev in range(aux_count)]
        shares.append(lax.ppermute(more if turn == half_count else tables, "aux", turned))
    other = shares[half_count][:, slots:]
    shares[half_count] = shares[half_count][:, :slots]
    tables = jnp.zeros((aux_count,) + tables.shape, jnp.int32)
    owners = jnp.arange(aux_count)[:, None, None]
    for turn, share in enumerate(shares):
        owner = lax.rem(place[1] + aux_count - turn, aux_count)
        tables = jnp.where(owners == owner, share[None], tables)
    tables = tables.transpose(1, 0, 2).reshape(pair_dev, all_slots)
    send = pair_places(tables, pair_dev, dev_count, False)

    other_orbits = [other[:, :slots].reshape(-1), other[:, slots:].reshape(-1)]
    other_orbits = jnp.concatenate(other_orbits + [pair_orbits.reshape(-1)])
    other_send, other_read = pair_places(shares[half_count], pair_dev, dev_count, True)
    lower = [part for dev in range(half_count) for part in (dev, dev + half_count)]
    upper = [part for dev in range(half_count) for part in (dev + half_count, dev)]
    by_part = send.reshape(dev_count, aux_count, per_dev)
    half_send = jnp.where(
        place[1] < half_count,
        jnp.stack([by_part[:, part] for part in lower], axis=1),
        jnp.stack([by_part[:, part] for part in upper], axis=1),
    ).reshape(-1)

    places = dev_count * all_slots * MOST
    packed = shape((places, rows, width), bf16)
    pack_scratch = [pltpu.VMEM(packed.shape, bf16), pltpu.SemaphoreType.DMA((dev_count,))]
    kept, half, amps_out = pl.pallas_call(
        start_kernel,
        out_shape=(
            shape(amps_in.shape, f32),
            shape(amps_in.shape, bf16),
            packed,
        ),
        in_specs=[SMEM, SMEM, SMEM, VMEM],
        out_specs=(VMEM, VMEM, HBM),
        scratch_shapes=pack_scratch,
        compiler_params=params(amps_in, amps_in, amps_in, packed),
        cost_estimate=FREE,
        name="mask_and_pack",
    )(place, send, pno_count, amps_in)

    def exchange(packed):
        packed = packed.reshape(dev_count * aux_count, per_dev, rows, width)
        got = lax.all_to_all(packed, ("pairs", "aux"), split_axis=0, concat_axis=0, tiled=True)
        return got.reshape(dev_count, aux_count, per_dev, rows, width)

    ahead = slice(1, dev_count // 2 + 1)
    amps_out, coef_far[ahead] = lax.optimization_barrier((amps_out, coef_far[ahead]))
    amps_far = exchange(amps_out)

    block = 8
    by_pair = lambda *dims: pl.BlockSpec((block,) + dims, lambda step: (step,) + (0,) * len(dims))
    fit = fit_left.shape[2]
    wide = by_pair(width, width)
    slab = by_pair(rows, width)
    line = by_pair(1, width)
    tall = pl.BlockSpec((aux_count, block, rows, width), lambda step: (0, step, 0, 0))
    by_rows = shape((aux_count, pair_dev, rows, width), f32)
    start, scale, mine, energy = pl.pallas_call(
        prepare_kernel,
        grid=(pair_dev // block,),
        out_shape=(
            by_rows,
            shape(amps_in.shape, f32),
            shape(amps_in.shape, f32),
            shape((pair_dev, 1, width), f32),
        ),
        in_specs=[SMEM, SMEM, SMEM, VMEM, by_pair(width, fit), by_pair(width, fit), wide, slab, slab],
        out_specs=(tall, slab, slab, line),
        compiler_params=pltpu.CompilerParams(vmem_limit_bytes=WIDE_BYTES),
        cost_estimate=FREE,
        name="integrals",
    )(place, pno_count, orbits, occ_fock, fit_left, fit_right, virt_fock, kept, half)

    own_shape = shape((items, width, pno_coef.shape[1]), bf16)

    def own_coef(read):
        return pl.pallas_call(
            functools.partial(own_coef_kernel, slots),
            out_shape=own_shape,
            in_specs=[SMEM, SMEM, VMEM],
            out_specs=VMEM,
            compiler_params=params(pno_coef, own_shape),
            name="own_coef",
        )(place, read, pno_coef)

    def projected(turns, read, own, arrived):
        out = shape((len(turns) * per_dev, width, width), bf16)
        return pl.pallas_call(
            functools.partial(projector_kernel, turns),
            out_shape=out,
            in_specs=[SMEM, SMEM] + [VMEM] * (1 + len(turns)),
            out_specs=VMEM,
            compiler_params=params(own, out, *arrived),
            name="projectors",
        )(place, read, own, *arrived)

    early = tuple(range(dev_count - 1)[ahead])
    groups = (early, tuple(turn for turn in range(dev_count - 1) if turn not in early))
    own = own_coef(coef_read)
    projectors = [
        projected(turns, coef_read, own, [coef_far[turn] for turn in turns]) for turns in groups
    ]

    def coupled(amps_far, start, tables, projectors, scaled):
        if scaled:
            out, extra = shape((aux_count, pair_dev + 1, rows, width), f32), shape((1, width), f32)
        else:
            out, extra = shape(start.shape, bf16), shape(amps_in.shape, f32)
        held = shape((dev_count, aux_count) + amps_far.shape[2:], bf16)
        return pl.pallas_call(
            functools.partial(coupling_kernel, groups, scaled),
            out_shape=(out, extra),
            in_specs=[SMEM] * (1 + len(tables)) + [VMEM] * (1 + len(projectors)) + [HBM] * 2,
            out_specs=(VMEM, VMEM),
            scratch_shapes=[
                pltpu.VMEM(held.shape, bf16),
                pltpu.SemaphoreType.DMA((dev_count - 1,)),
                pltpu.SemaphoreType.DMA((aux_count,)),
            ]
            + ([] if scaled else [pltpu.VMEM(start.shape, f32)]),
            compiler_params=params(out, amps_in, start, held, *projectors),
            name="coupling",
        )(place, *tables, occ_fock, *projectors, amps_far, start)

    tables = [coef_read, orbits]
    total, shrink = coupled(amps_far, start, tables, projectors, True)
    to_sum = (total * shrink).astype(jnp.float16)
    to_sum, other_send = lax.optimization_barrier((to_sum, other_send))
    other_out = list(packed_coef(other_send))
    other_far = [None] * len(other_out)

    def send_turns(turns):
        for turn in turns:
            pairs = [(dev, dev ^ (turn + 1)) for dev in range(dev_count)]
            other_far[turn] = lax.ppermute(other_out[turn], "pairs", pairs)

    first, second = groups
    send_turns(first)
    tied = ([other_out[turn] for turn in second], [other_far[turn] for turn in first])
    waiting, arrived = lax.optimization_barrier(tied)
    for turn, packed_turn in zip(second, waiting):
        other_out[turn] = packed_turn
    for turn, arrived_turn in zip(first, arrived):
        other_far[turn] = arrived_turn
    send_turns(second)
    got = lax.all_to_all(to_sum, "aux", split_axis=0, concat_axis=0, tiled=True)
    foreign = (jnp.arange(aux_count) != place[1])[:, None, None, None]
    grow = jnp.where(foreign, jnp.exp2(got[:, pair_dev:, :1].astype(f32)), 0.0)
    sums = lax.dynamic_index_in_dim(total, place[1], 0, keepdims=False)[:pair_dev]
    for turn in range(aux_count):
        sums = sums + got[turn, :pair_dev].astype(f32) * grow[turn]

    every = tuple(range(dev_count - 1))
    sums, other_far = lax.optimization_barrier((sums, other_far))
    other_projectors = projected(every, other_read, own_coef(other_read), other_far)

    before = half
    kept, half, amps_out = pl.pallas_call(
        first_update_kernel,
        out_shape=(
            shape(amps_in.shape, f32),
            shape(amps_in.shape, bf16),
            packed,
        ),
        in_specs=[SMEM] + [VMEM] * 4,
        out_specs=(VMEM, VMEM, HBM),
        scratch_shapes=pack_scratch,
        compiler_params=params(amps_in, amps_in, amps_in, amps_in, amps_in, amps_in, packed),
        name="first_update",
    )(half_send, sums, mine, scale, kept)

    halves = [
        [dev * aux_count + part for dev in range(dev_count) for part in range(first, last)]
        for first, last in ((0, half_count), (half_count, aux_count))
    ]
    amps_far = amps_out.reshape(dev_count * half_count, 2 * per_dev, rows, width)
    amps_far = lax.all_to_all(
        amps_far, ("pairs", "aux"), split_axis=0, concat_axis=0, axis_index_groups=halves, tiled=True
    ).reshape(dev_count, half_count, 2 * per_dev, rows, width)

    start, own = pl.pallas_call(
        between_kernel,
        grid=(pair_dev // block,),
        out_shape=(by_rows, shape(amps_in.shape, f32)),
        in_specs=[SMEM, line, wide, slab, slab, slab, slab, tall, tall],
        out_specs=(tall, slab),
        compiler_params=params(*[shape((2 * block,) + dims, f32) for dims in ((width, 3 * width), (rows, 6 * width))]),
        cost_estimate=pl.CostEstimate(
            flops=6 * pair_dev * width * width * rows,
            bytes_accessed=pair_dev * width * width * 10,
            transcendentals=0,
        ),
        name="between",
    )(place, energy, virt_fock, kept, half, before, sums, start, total)

    tables += [other_read, other_orbits]
    projectors.append(other_projectors)
    to_sum, mine = coupled(amps_far, start, tables, projectors, False)
    got = lax.all_to_all(to_sum, "aux", split_axis=0, concat_axis=0, tiled=True)

    return pl.pallas_call(
        last_update_kernel,
        out_shape=shape(amps_in.shape, f32),
        in_specs=[SMEM] + [VMEM] * 5,
        out_specs=VMEM,
        compiler_params=params(got, mine, own, scale, kept, amps_in),
        name="last_update",
    )(place, got, mine, own, scale, kept)


def solution(mesh):
    return jax.shard_map(
        per_device,
        mesh=mesh,
        in_specs=(
            P("pairs", None),
            P("pairs"),
            P("pairs", "aux"),
            P("pairs", "aux"),
            P("pairs", "aux"),
            P(),
            P("pairs", None, "aux"),
            P("pairs", None, "aux"),
            P("pairs", None, None),
            P("pairs", None, None),
            P("pairs", "aux", None),
        ),
        out_specs=P("pairs", "aux", None),
        check_vma=False,
    )
```

```python
import functools

import jax
import jax.numpy as jnp
from jax import lax
from jax.experimental import pallas as pl
from jax.experimental.pallas import tpu as pltpu
from jax.sharding import PartitionSpec as P

MOST = 2
SPARE_BYTES = 3 * 1024 * 1024
WIDE_BYTES = 48 * 1024 * 1024

SMEM = pl.BlockSpec(memory_space=pltpu.SMEM)
VMEM = pl.BlockSpec(memory_space=pltpu.VMEM)
HBM = pl.BlockSpec(memory_space=pltpu.HBM)
FREE = pl.CostEstimate(flops=0, bytes_accessed=0, transcendentals=0)


def dot(left, right, over_left, over_right):
    return lax.dot_general(
        left, right, (((over_left,), (over_right,)), ((), ())), preferred_element_type=jnp.float32
    )


def params(*arrays):
    held = sum(array.size * array.dtype.itemsize for array in arrays)
    needed = held + held // 8 + SPARE_BYTES
    return pltpu.CompilerParams(vmem_limit_bytes=max(needed, WIDE_BYTES))


def pair_places(partner, pair_dev, dev_count, arrival):
    slots = partner.shape[1]
    owner = jnp.where(partner >= 0, partner // pair_dev, -1)
    own_id = jnp.broadcast_to(jnp.arange(pair_dev, dtype=jnp.int32)[:, None], partner.shape)
    far_key = (partner - owner * pair_dev) * pair_dev + own_id
    none = pair_dev * pair_dev
    devs = jnp.arange(dev_count, dtype=jnp.int32)[None, :, None]
    hit = owner[:, None, :] == devs

    def ranked(key):
        left = jnp.where(hit, key[:, None, :], none)
        found = []
        for _ in range(MOST):
            least = jnp.min(left, axis=0)
            found.append(least)
            left = jnp.where(left == least[None], none, left)
        return jnp.stack(found, axis=-1).reshape(-1)

    send = ranked(own_id)
    send = jnp.where(send < none, send, 0)
    if not arrival:
        return send
    read = ranked(far_key)
    return send, jnp.where(read < none, lax.rem(read, pair_dev), -1)


def pack_rows(send_ref, half_ref, out_ref, held, sems):
    chunk = held.shape[0] // sems.shape[0]

    def store(turn):
        at = pl.ds(pl.multiple_of(turn * chunk, chunk), chunk)
        return pltpu.make_async_copy(held.at[at], out_ref.at[at], sems.at[turn])

    def body(turn, carry):
        for item in range(chunk):
            place = turn * chunk + item
            held[place] = half_ref[send_ref[place]]
        store(turn).start()
        return carry

    def finish(turn, carry):
        store(turn).wait()
        return carry

    lax.fori_loop(0, sems.shape[0], body, 0)
    lax.fori_loop(0, sems.shape[0], finish, 0)


def start_kernel(
    place_ref, send_ref, count_ref, amps_ref, kept_ref, half_ref, out_ref, held, sems
):
    pairs, rows, width = amps_ref.shape
    row_id = lax.broadcasted_iota(jnp.int32, (rows, width), 0) + place_ref[1] * rows
    col_id = lax.broadcasted_iota(jnp.int32, (rows, width), 1)
    last = jnp.maximum(row_id, col_id)

    def body(pair, carry):
        kept = jnp.where(last < count_ref[pair], amps_ref[pair], 0.0)
        kept_ref[pair] = kept
        half_ref[pair] = kept.astype(jnp.bfloat16)
        return carry

    lax.fori_loop(0, pairs, body, 0, unroll=4)
    pack_rows(send_ref, half_ref, out_ref, held, sems)


def coef_kernel(slots, place_ref, send_ref, coef_ref, *rest):
    outs, (held, in_sems, out_sems) = rest[:-3], rest[-3:]
    per_dev = slots * MOST

    def fetch(turn, item):
        far = place_ref[0] ^ (turn + 1)
        pair = send_ref[far * per_dev + item]
        place = turn * per_dev + item
        return pltpu.make_async_copy(coef_ref.at[pair], held.at[place], in_sems.at[place])

    def store(turn):
        return pltpu.make_async_copy(
            held.at[pl.ds(turn * per_dev, per_dev)], outs[turn], out_sems.at[turn]
        )

    for turn in range(len(outs)):
        for item in range(per_dev):
            fetch(turn, item).start()
    for turn in range(len(outs)):
        for item in range(per_dev):
            fetch(turn, item).wait()
        store(turn).start()
    for turn in range(len(outs)):
        store(turn).wait()


def put_rows(out_ref, pair, value):
    rows = out_ref.shape[2]
    for part in range(out_ref.shape[0]):
        out_ref[part, pair] = value[part * rows : (part + 1) * rows]


def element(matrix_ref, row, column):
    line = matrix_ref[pl.ds(row, 1), :]
    at = lax.broadcasted_iota(jnp.int32, line.shape, 1) == column
    return jnp.sum(jnp.where(at, line, 0.0), axis=1, keepdims=True)


def left_part(fock_rows, half_rows):
    return dot(fock_rows, half_rows, 0, 0)


def prepare_kernel(
    place_ref, count_ref, orbit_ref, occ_ref, left_ref, right_ref, fock_ref, kept_ref, half_ref,
    part_ref, scale_ref, own_ref, energy_ref,
):
    block, rows, width = kept_ref.shape
    first = pl.program_id(0) * block
    row_start = pl.multiple_of(place_ref[1] * rows, rows)
    row_id = lax.broadcasted_iota(jnp.int32, (rows, width), 0) + row_start
    col_id = lax.broadcasted_iota(jnp.int32, (rows, width), 1)
    last = jnp.maximum(row_id, col_id)
    eye_rows = row_id == col_id
    eye = lax.broadcasted_iota(jnp.int32, (width, width), 0) == lax.broadcasted_iota(
        jnp.int32, (width, width), 1
    )
    for pair in range(block):
        at = orbit_ref.shape[0] - 2 * (count_ref.shape[0] - first - pair)
        orbit, other = orbit_ref[at], orbit_ref[at + 1]
        energy = element(occ_ref, orbit, orbit) + element(occ_ref, other, other)
        energy_ref[pair] = jnp.broadcast_to(energy, (1, width))
        fock = fock_ref[pair]
        fock_rows = fock_ref[pair, pl.ds(row_start, rows), :]
        half = half_ref[pair]
        fitted = dot(left_ref[pair], right_ref[pair], 1, 1)
        put_rows(part_ref, pair, fitted + left_part(fock_rows, half))
        own_ref[pair] = dot(half, fock, 1, 0) - energy * kept_ref[pair]
        diag_cols = jnp.sum(jnp.where(eye, fock.astype(jnp.float32), 0.0), axis=0, keepdims=True)
        diag_rows = jnp.sum(
            jnp.where(eye_rows, fock_rows.astype(jnp.float32), 0.0), axis=1, keepdims=True
        )
        denominator = diag_rows + diag_cols - energy
        scale_ref[pair] = jnp.where(last < count_ref[first + pair], 1.0 / denominator, 0.0)


def any_live(read_ref, first, per_dev, rank):
    most = read_ref[first + rank]
    for item in range(rank + MOST, per_dev, MOST):
        most = jnp.maximum(most, read_ref[first + item])
    return most >= 0


def own_coef_kernel(slots, place_ref, read_ref, coef_ref, out_ref):
    per_dev = slots * MOST

    def body(turn, carry):
        far = place_ref[0] ^ (turn + 1)
        for item in range(per_dev):
            pair = jnp.maximum(read_ref[far * per_dev + item], 0)
            out_ref[turn * per_dev + item] = coef_ref[pair].T
        return carry

    lax.fori_loop(0, out_ref.shape[0] // per_dev, body, 0)


def projector_kernel(turns, place_ref, read_ref, own_ref, *rest):
    arrived, out_ref = rest[:-1], rest[-1]
    per_dev = arrived[0].shape[0]

    def rank_items(place, turn, rank):
        for item in range(rank, per_dev, MOST):
            own = own_ref[turn * per_dev + item]
            out_ref[place * per_dev + item] = dot(own, arrived[place][item], 1, 0).astype(
                jnp.bfloat16
            )

    for place, turn in enumerate(turns):
        far = place_ref[0] ^ (turn + 1)
        for rank in range(MOST):
            pl.when(any_live(read_ref, far * per_dev, per_dev, rank))(
                functools.partial(rank_items, place, turn, rank)
            )


def add_coupling(sets, place_ref, occ_ref, fetch, amps_ref, part_ref):
    parts, rows, width = part_ref.shape[0], part_ref.shape[2], part_ref.shape[3]
    per_dev = amps_ref.shape[2] // len(sets)
    slots = per_dev // MOST
    pairs = sets[0][1].shape[0] // (2 * slots + 2)
    side_at, pair_at = pairs * slots, 2 * pairs * slots

    def body(turn, place, proj_ref, read_ref, orbit_ref, offset):
        far = place_ref[0] ^ (turn + 1)
        if offset == 0:
            fetch(turn).wait()

        def rank_terms(rank):
            terms = []
            for item in range(rank, per_dev, MOST):
                pair = read_ref[far * per_dev + item]
                safe = jnp.maximum(pair, 0)
                entry = safe * slots + item // MOST
                orbit = orbit_ref[pair_at + 2 * safe + orbit_ref[side_at + entry]]
                coupled = element(occ_ref, orbit_ref[entry], orbit)
                weight = jnp.where(pair >= 0, -coupled, 0.0)
                proj = proj_ref[place * per_dev + item]
                amps = amps_ref[far, :, offset + item].reshape(width, width)
                mixed = dot(proj, amps, 1, 0).astype(jnp.bfloat16)
                terms.append((safe, weight * dot(mixed, proj, 1, 1)))
            for safe, term in terms:
                for part in range(parts):
                    part_ref[part, safe] += term[part * rows : (part + 1) * rows]

        for rank in range(MOST):
            pl.when(any_live(read_ref, far * per_dev, per_dev, rank))(
                functools.partial(rank_terms, rank)
            )

    for number, (read_ref, orbit_ref, groups) in enumerate(sets):
        for turns, proj_ref in groups:
            later = turns[min(1, len(turns) - 1)] - min(1, len(turns) - 1)

            def step(place, carry, first=turns[0], later=later, proj_ref=proj_ref):
                turn = jnp.where(place == 0, first, place + later)
                body(turn, place, proj_ref, read_ref, orbit_ref, number * per_dev)
                return carry

            lax.fori_loop(0, len(turns), step, 0)


def coupling_kernel(groups, scaled, place_ref, *refs):
    set_count = 1 if scaled else 2
    tables, refs = refs[: 2 * set_count], refs[2 * set_count :]
    occ_ref, early_ref, late_ref = refs[:3]
    sets = [(tables[0], tables[1], list(zip(groups, (early_ref, late_ref))))]
    if not scaled:
        every = tuple(range(sum(len(turns) for turns in groups)))
        sets.append((tables[2], tables[3], [(every, refs[3])]))
    amps_hbm, start_hbm, out_ref, extra_ref, amps_ref, amps_sems, start_sem, *rest = refs[
        2 + set_count :
    ]
    part_ref = out_ref if scaled else rest[0]
    parts, pairs, rows, width = start_hbm.shape
    given = amps_hbm.shape[1]
    first_row = (place_ref[1] // given) * given

    def fetch(turn):
        far = place_ref[0] ^ (turn + 1)
        return pltpu.make_async_copy(
            amps_hbm.at[far], amps_ref.at[far, pl.ds(first_row, given)], amps_sems.at[turn]
        )

    loads = [
        pltpu.make_async_copy(
            start_hbm.at[part], part_ref.at[part, pl.ds(0, pairs)], start_sem.at[part]
        )
        for part in range(parts)
    ]
    for load in loads:
        load.start()
    for turns in groups:
        for turn in turns:
            fetch(turn).start()
    if given < parts:
        blank = jnp.zeros(amps_ref.shape[2:], amps_ref.dtype)

        def clear(far, carry):
            for row in range(parts - given):
                amps_ref[far, lax.rem(first_row + given + row, parts)] = blank
            return carry

        lax.fori_loop(0, amps_ref.shape[0], clear, 0)
    for load in loads:
        load.wait()
    add_coupling(sets, place_ref, occ_ref, fetch, amps_ref, part_ref)
    if not scaled:

        def body(pair, carry):
            for part in range(parts):
                out_ref[part, pair] = part_ref[part, pair].astype(out_ref.dtype)
            extra_ref[pair] = part_ref[place_ref[1], pair]
            return carry

        lax.fori_loop(0, pairs, body, 0, unroll=4)
        return

    def body(pair, most):
        for part in range(parts):
            most = jnp.maximum(most, jnp.abs(part_ref[part, pair]))
        return most

    most = lax.fori_loop(0, pairs, body, jnp.zeros((rows, width), jnp.float32), unroll=4)
    most = jnp.max(jnp.max(most, axis=0, keepdims=True), axis=1, keepdims=True)
    power = jnp.maximum(jnp.ceil(jnp.log2(jnp.maximum(most, 1.0)) - 15.0), 0.0)
    for part in range(parts):
        out_ref[part, pairs] = jnp.broadcast_to(power * jnp.exp2(power), (rows, width))
    extra_ref[...] = jnp.broadcast_to(jnp.exp2(-power), (1, width))


def first_update_kernel(
    send_ref, sum_ref, own_ref, scale_ref, kept_ref, new_ref, half_ref, out_ref, held, sems
):
    def body(pair, carry):
        new = kept_ref[pair] - (sum_ref[pair] + own_ref[pair]) * scale_ref[pair]
        new_ref[pair] = new
        half_ref[pair] = new.astype(jnp.bfloat16)
        return carry

    lax.fori_loop(0, new_ref.shape[0], body, 0, unroll=4)
    pack_rows(send_ref, half_ref, out_ref, held, sems)


def between_kernel(
    place_ref, energy_ref, fock_ref, kept_ref, half_ref, before_ref, sum_ref, start_ref, old_ref,
    part_ref, own_ref,
):
    block, rows, width = kept_ref.shape
    row_start = pl.multiple_of(place_ref[1] * rows, rows)
    for pair in range(block):
        half = half_ref[pair]
        fock_rows = fock_ref[pair, pl.ds(row_start, rows), :]
        change = left_part(fock_rows, half) - left_part(fock_rows, before_ref[pair])
        for part in range(part_ref.shape[0]):
            part_ref[part, pair] = (
                start_ref[part, pair] - old_ref[part, pair] + change[part * rows : (part + 1) * rows]
            )
        own_ref[pair] = (
            dot(half, fock_ref[pair], 1, 0)
            - energy_ref[pair] * kept_ref[pair]
            + sum_ref[pair]
        )


def last_update_kernel(place_ref, got_ref, mine_ref, own_ref, scale_ref, kept_ref, new_ref):
    def body(pair, carry):
        total = mine_ref[pair]
        for turn in range(1, got_ref.shape[0]):
            part = lax.rem(place_ref[1] + turn, got_ref.shape[0])
            total = total + got_ref[part, pair].astype(jnp.float32)
        new_ref[pair] = kept_ref[pair] - (total + own_ref[pair]) * scale_ref[pair]
        return carry

    lax.fori_loop(0, new_ref.shape[0], body, 0, unroll=4)


def shape(dims, dtype):
    return jax.ShapeDtypeStruct(tuple(dims), dtype)


def per_device(
    pair_orbits,
    pno_count,
    partner,
    couple_orbit,
    couple_side,
    occ_fock,
    fit_left,
    fit_right,
    pno_coef,
    virt_fock,
    amps_in,
):
    pair_dev = pno_count.shape[0]
    width = virt_fock.shape[1]
    rows = amps_in.shape[1]
    slots = partner.shape[1]
    dev_count = lax.axis_size("pairs")
    aux_count = lax.axis_size("aux")
    all_slots = slots * aux_count
    per_dev = slots * MOST
    items = (dev_count - 1) * per_dev
    bf16, f32 = jnp.bfloat16, jnp.float32
    place = jnp.stack([lax.axis_index("pairs"), lax.axis_index("aux")]).astype(jnp.int32)

    orbits = [couple_orbit.reshape(-1), couple_side.reshape(-1), pair_orbits.reshape(-1)]
    orbits = jnp.concatenate(orbits)
    coef_send, coef_read = pair_places(partner, pair_dev, dev_count, True)

    def packed_coef(send):
        return pl.pallas_call(
            functools.partial(coef_kernel, slots),
            out_shape=tuple(
                shape((per_dev,) + pno_coef.shape[1:], bf16) for _ in range(dev_count - 1)
            ),
            in_specs=[SMEM, SMEM, HBM],
            out_specs=tuple(HBM for _ in range(dev_count - 1)),
            scratch_shapes=[
                pltpu.VMEM((items,) + pno_coef.shape[1:], bf16),
                pltpu.SemaphoreType.DMA((items,)),
                pltpu.SemaphoreType.DMA((dev_count - 1,)),
            ],
            compiler_params=params(shape((items,) + pno_coef.shape[1:], bf16)),
            cost_estimate=FREE,
            name="pack_coef",
        )(place, send, pno_coef)

    def sent_coef(coef_out):
        return [
            lax.ppermute(packed, "pairs", [(dev, dev ^ (turn + 1)) for dev in range(dev_count)])
            for turn, packed in enumerate(coef_out)
        ]

    coef_out = packed_coef(coef_send)
    tables = partner
    tables, coef_out = lax.optimization_barrier((tables, coef_out))
    coef_far = sent_coef(coef_out)
    half_count = aux_count // 2
    more = jnp.concatenate([tables, couple_orbit, couple_side], axis=1)
    shares = [tables]
    for turn in range(1, aux_count):
        turned = [(dev, (dev + turn) % aux_count) for dev in range(aux_count)]
        shares.append(lax.ppermute(more if turn == half_count else tables, "aux", turned))
    other = shares[half_count][:, slots:]
    shares[half_count] = shares[half_count][:, :slots]
    tables = jnp.zeros((aux_count,) + tables.shape, jnp.int32)
    owners = jnp.arange(aux_count)[:, None, None]
    for turn, share in enumerate(shares):
        owner = lax.rem(place[1] + aux_count - turn, aux_count)
        tables = jnp.where(owners == owner, share[None], tables)
    tables = tables.transpose(1, 0, 2).reshape(pair_dev, all_slots)
    send = pair_places(tables, pair_dev, dev_count, False)

    other_orbits = [other[:, :slots].reshape(-1), other[:, slots:].reshape(-1)]
    other_orbits = jnp.concatenate(other_orbits + [pair_orbits.reshape(-1)])
    other_send, other_read = pair_places(shares[half_count], pair_dev, dev_count, True)
    lower = [part for dev in range(half_count) for part in (dev, dev + half_count)]
    upper = [part for dev in range(half_count) for part in (dev + half_count, dev)]
    by_part = send.reshape(dev_count, aux_count, per_dev)
    half_send = jnp.where(
        place[1] < half_count,
        jnp.stack([by_part[:, part] for part in lower], axis=1),
        jnp.stack([by_part[:, part] for part in upper], axis=1),
    ).reshape(-1)

    places = dev_count * all_slots * MOST
    packed = shape((places, rows, width), bf16)
    pack_scratch = [pltpu.VMEM(packed.shape, bf16), pltpu.SemaphoreType.DMA((dev_count,))]
    kept, half, amps_out = pl.pallas_call(
        start_kernel,
        out_shape=(
            shape(amps_in.shape, f32),
            shape(amps_in.shape, bf16),
            packed,
        ),
        in_specs=[SMEM, SMEM, SMEM, VMEM],
        out_specs=(VMEM, VMEM, HBM),
        scratch_shapes=pack_scratch,
        compiler_params=params(amps_in, amps_in, amps_in, packed),
        cost_estimate=FREE,
        name="mask_and_pack",
    )(place, send, pno_count, amps_in)

    def exchange(packed):
        packed = packed.reshape(dev_count * aux_count, per_dev, rows, width)
        got = lax.all_to_all(packed, ("pairs", "aux"), split_axis=0, concat_axis=0, tiled=True)
        return got.reshape(dev_count, aux_count, per_dev, rows, width)

    ahead = slice(1, dev_count // 2 + 1)
    leading = slice(1, dev_count // 2 + 1, 2)
    amps_out, coef_far[leading] = lax.optimization_barrier((amps_out, coef_far[leading]))
    amps_far = exchange(amps_out)

    block = 8
    by_pair = lambda *dims: pl.BlockSpec((block,) + dims, lambda step: (step,) + (0,) * len(dims))
    fit = fit_left.shape[2]
    wide = by_pair(width, width)
    slab = by_pair(rows, width)
    line = by_pair(1, width)
    tall = pl.BlockSpec((aux_count, block, rows, width), lambda step: (0, step, 0, 0))
    by_rows = shape((aux_count, pair_dev, rows, width), f32)
    start, scale, mine, energy = pl.pallas_call(
        prepare_kernel,
        grid=(pair_dev // block,),
        out_shape=(
            by_rows,
            shape(amps_in.shape, f32),
            shape(amps_in.shape, f32),
            shape((pair_dev, 1, width), f32),
        ),
        in_specs=[SMEM, SMEM, SMEM, VMEM, by_pair(width, fit), by_pair(width, fit), wide, slab, slab],
        out_specs=(tall, slab, slab, line),
        compiler_params=pltpu.CompilerParams(vmem_limit_bytes=WIDE_BYTES),
        cost_estimate=FREE,
        name="integrals",
    )(place, pno_count, orbits, occ_fock, fit_left, fit_right, virt_fock, kept, half)

    own_shape = shape((items, width, pno_coef.shape[1]), bf16)

    def own_coef(read):
        return pl.pallas_call(
            functools.partial(own_coef_kernel, slots),
            out_shape=own_shape,
            in_specs=[SMEM, SMEM, VMEM],
            out_specs=VMEM,
            compiler_params=params(pno_coef, own_shape),
            name="own_coef",
        )(place, read, pno_coef)

    def projected(turns, read, own, arrived):
        out = shape((len(turns) * per_dev, width, width), bf16)
        return pl.pallas_call(
            functools.partial(projector_kernel, turns),
            out_shape=out,
            in_specs=[SMEM, SMEM] + [VMEM] * (1 + len(turns)),
            out_specs=VMEM,
            compiler_params=params(own, out, *arrived),
            name="projectors",
        )(place, read, own, *arrived)

    early = tuple(range(dev_count - 1)[ahead])
    groups = (early, tuple(turn for turn in range(dev_count - 1) if turn not in early))
    own = own_coef(coef_read)
    projectors = [
        projected(turns, coef_read, own, [coef_far[turn] for turn in turns]) for turns in groups
    ]

    def coupled(amps_far, start, tables, projectors, scaled):
        if scaled:
            out, extra = shape((aux_count, pair_dev + 1, rows, width), f32), shape((1, width), f32)
        else:
            out, extra = shape(start.shape, bf16), shape(amps_in.shape, f32)
        held = shape((dev_count, aux_count) + amps_far.shape[2:], bf16)
        return pl.pallas_call(
            functools.partial(coupling_kernel, groups, scaled),
            out_shape=(out, extra),
            in_specs=[SMEM] * (1 + len(tables)) + [VMEM] * (1 + len(projectors)) + [HBM] * 2,
            out_specs=(VMEM, VMEM),
            scratch_shapes=[
                pltpu.VMEM(held.shape, bf16),
                pltpu.SemaphoreType.DMA((dev_count - 1,)),
                pltpu.SemaphoreType.DMA((aux_count,)),
            ]
            + ([] if scaled else [pltpu.VMEM(start.shape, f32)]),
            compiler_params=params(out, amps_in, start, held, *projectors),
            name="coupling",
        )(place, *tables, occ_fock, *projectors, amps_far, start)

    tables = [coef_read, orbits]
    total, shrink = coupled(amps_far, start, tables, projectors, True)
    to_sum = (total * shrink).astype(jnp.float16)
    to_sum, other_send = lax.optimization_barrier((to_sum, other_send))
    other_out = list(packed_coef(other_send))
    other_far = [None] * len(other_out)

    def send_turns(turns):
        for turn in turns:
            pairs = [(dev, dev ^ (turn + 1)) for dev in range(dev_count)]
            other_far[turn] = lax.ppermute(other_out[turn], "pairs", pairs)

    first, second = groups
    send_turns(first)
    tied = ([other_out[turn] for turn in second], [other_far[turn] for turn in first])
    waiting, arrived = lax.optimization_barrier(tied)
    for turn, packed_turn in zip(second, waiting):
        other_out[turn] = packed_turn
    for turn, arrived_turn in zip(first, arrived):
        other_far[turn] = arrived_turn
    send_turns(second)
    got = lax.all_to_all(to_sum, "aux", split_axis=0, concat_axis=0, tiled=True)
    foreign = (jnp.arange(aux_count) != place[1])[:, None, None, None]
    grow = jnp.where(foreign, jnp.exp2(got[:, pair_dev:, :1].astype(f32)), 0.0)
    sums = lax.dynamic_index_in_dim(total, place[1], 0, keepdims=False)[:pair_dev]
    for turn in range(aux_count):
        sums = sums + got[turn, :pair_dev].astype(f32) * grow[turn]

    every = tuple(range(dev_count - 1))
    sums, other_far = lax.optimization_barrier((sums, other_far))
    other_projectors = projected(every, other_read, own_coef(other_read), other_far)

    before = half
    kept, half, amps_out = pl.pallas_call(
        first_update_kernel,
        out_shape=(
            shape(amps_in.shape, f32),
            shape(amps_in.shape, bf16),
            packed,
        ),
        in_specs=[SMEM] + [VMEM] * 4,
        out_specs=(VMEM, VMEM, HBM),
        scratch_shapes=pack_scratch,
        compiler_params=params(amps_in, amps_in, amps_in, amps_in, amps_in, amps_in, packed),
        name="first_update",
    )(half_send, sums, mine, scale, kept)

    halves = [
        [dev * aux_count + part for dev in range(dev_count) for part in range(first, last)]
        for first, last in ((0, half_count), (half_count, aux_count))
    ]
    amps_far = amps_out.reshape(dev_count * half_count, 2 * per_dev, rows, width)
    amps_far = lax.all_to_all(
        amps_far, ("pairs", "aux"), split_axis=0, concat_axis=0, axis_index_groups=halves, tiled=True
    ).reshape(dev_count, half_count, 2 * per_dev, rows, width)

    start, own = pl.pallas_call(
        between_kernel,
        grid=(pair_dev // block,),
        out_shape=(by_rows, shape(amps_in.shape, f32)),
        in_specs=[SMEM, line, wide, slab, slab, slab, slab, tall, tall],
        out_specs=(tall, slab),
        compiler_params=params(*[shape((2 * block,) + dims, f32) for dims in ((width, 3 * width), (rows, 6 * width))]),
        cost_estimate=pl.CostEstimate(
            flops=6 * pair_dev * width * width * rows,
            bytes_accessed=pair_dev * width * width * 10,
            transcendentals=0,
        ),
        name="between",
    )(place, energy, virt_fock, kept, half, before, sums, start, total)

    tables += [other_read, other_orbits]
    projectors.append(other_projectors)
    to_sum, mine = coupled(amps_far, start, tables, projectors, False)
    got = lax.all_to_all(to_sum, "aux", split_axis=0, concat_axis=0, tiled=True)

    return pl.pallas_call(
        last_update_kernel,
        out_shape=shape(amps_in.shape, f32),
        in_specs=[SMEM] + [VMEM] * 5,
        out_specs=VMEM,
        compiler_params=params(got, mine, own, scale, kept, amps_in),
        name="last_update",
    )(place, got, mine, own, scale, kept)


def solution(mesh):
    return jax.shard_map(
        per_device,
        mesh=mesh,
        in_specs=(
            P("pairs", None),
            P("pairs"),
            P("pairs", "aux"),
            P("pairs", "aux"),
            P("pairs", "aux"),
            P(),
            P("pairs", None, "aux"),
            P("pairs", None, "aux"),
            P("pairs", None, None),
            P("pairs", None, None),
            P("pairs", "aux", None),
        ),
        out_specs=P("pairs", "aux", None),
        check_vma=False,
    )
```

```python
import functools

import jax
import jax.numpy as jnp
from jax import lax
from jax.experimental import pallas as pl
from jax.experimental.pallas import tpu as pltpu
from jax.sharding import PartitionSpec as P

MOST = 2
SPARE_BYTES = 3 * 1024 * 1024
WIDE_BYTES = 48 * 1024 * 1024

SMEM = pl.BlockSpec(memory_space=pltpu.SMEM)
VMEM = pl.BlockSpec(memory_space=pltpu.VMEM)
HBM = pl.BlockSpec(memory_space=pltpu.HBM)
FREE = pl.CostEstimate(flops=0, bytes_accessed=0, transcendentals=0)


def dot(left, right, over_left, over_right):
    return lax.dot_general(
        left, right, (((over_left,), (over_right,)), ((), ())), preferred_element_type=jnp.float32
    )


def params(*arrays):
    held = sum(array.size * array.dtype.itemsize for array in arrays)
    needed = held + held // 8 + SPARE_BYTES
    return pltpu.CompilerParams(vmem_limit_bytes=max(needed, WIDE_BYTES))


def pair_places(partner, pair_dev, dev_count, arrival):
    slots = partner.shape[1]
    owner = jnp.where(partner >= 0, partner // pair_dev, -1)
    own_id = jnp.broadcast_to(jnp.arange(pair_dev, dtype=jnp.int32)[:, None], partner.shape)
    far_key = (partner - owner * pair_dev) * pair_dev + own_id
    none = pair_dev * pair_dev
    devs = jnp.arange(dev_count, dtype=jnp.int32)[None, :, None]
    hit = owner[:, None, :] == devs

    def ranked(key):
        left = jnp.where(hit, key[:, None, :], none)
        found = []
        for _ in range(MOST):
            least = jnp.min(left, axis=0)
            found.append(least)
            left = jnp.where(left == least[None], none, left)
        return jnp.stack(found, axis=-1).reshape(-1)

    send = ranked(own_id)
    send = jnp.where(send < none, send, 0)
    if not arrival:
        return send
    read = ranked(far_key)
    return send, jnp.where(read < none, lax.rem(read, pair_dev), -1)


def pack_rows(send_ref, half_ref, out_ref, held, sems):
    chunk = held.shape[0] // sems.shape[0]

    def store(turn):
        at = pl.ds(pl.multiple_of(turn * chunk, chunk), chunk)
        return pltpu.make_async_copy(held.at[at], out_ref.at[at], sems.at[turn])

    def body(turn, carry):
        for item in range(chunk):
            place = turn * chunk + item
            held[place] = half_ref[send_ref[place]]
        store(turn).start()
        return carry

    def finish(turn, carry):
        store(turn).wait()
        return carry

    lax.fori_loop(0, sems.shape[0], body, 0)
    lax.fori_loop(0, sems.shape[0], finish, 0)


def start_kernel(
    place_ref, send_ref, count_ref, amps_ref, kept_ref, half_ref, out_ref, held, sems
):
    pairs, rows, width = amps_ref.shape
    row_id = lax.broadcasted_iota(jnp.int32, (rows, width), 0) + place_ref[1] * rows
    col_id = lax.broadcasted_iota(jnp.int32, (rows, width), 1)
    last = jnp.maximum(row_id, col_id)

    def body(pair, carry):
        kept = jnp.where(last < count_ref[pair], amps_ref[pair], 0.0)
        kept_ref[pair] = kept
        half_ref[pair] = kept.astype(jnp.bfloat16)
        return carry

    lax.fori_loop(0, pairs, body, 0, unroll=4)
    pack_rows(send_ref, half_ref, out_ref, held, sems)


def coef_kernel(slots, place_ref, send_ref, coef_ref, *rest):
    outs, (held, in_sems, out_sems) = rest[:-3], rest[-3:]
    per_dev = slots * MOST

    def fetch(turn, item):
        far = place_ref[0] ^ (turn + 1)
        pair = send_ref[far * per_dev + item]
        place = turn * per_dev + item
        return pltpu.make_async_copy(coef_ref.at[pair], held.at[place], in_sems.at[place])

    def store(turn):
        return pltpu.make_async_copy(
            held.at[pl.ds(turn * per_dev, per_dev)], outs[turn], out_sems.at[turn]
        )

    for turn in range(len(outs)):
        for item in range(per_dev):
            fetch(turn, item).start()
    for turn in range(len(outs)):
        for item in range(per_dev):
            fetch(turn, item).wait()
        store(turn).start()
    for turn in range(len(outs)):
        store(turn).wait()


def put_rows(out_ref, pair, value):
    rows = out_ref.shape[2]
    for part in range(out_ref.shape[0]):
        out_ref[part, pair] = value[part * rows : (part + 1) * rows]


def element(matrix_ref, row, column):
    line = matrix_ref[pl.ds(row, 1), :]
    at = lax.broadcasted_iota(jnp.int32, line.shape, 1) == column
    return jnp.sum(jnp.where(at, line, 0.0), axis=1, keepdims=True)


def left_part(fock_rows, half_rows):
    return dot(fock_rows, half_rows, 0, 0)


def prepare_kernel(
    place_ref, count_ref, orbit_ref, occ_ref, left_ref, right_ref, fock_ref, kept_ref, half_ref,
    part_ref, scale_ref, own_ref, energy_ref,
):
    block, rows, width = kept_ref.shape
    first = pl.program_id(0) * block
    row_start = pl.multiple_of(place_ref[1] * rows, rows)
    row_id = lax.broadcasted_iota(jnp.int32, (rows, width), 0) + row_start
    col_id = lax.broadcasted_iota(jnp.int32, (rows, width), 1)
    last = jnp.maximum(row_id, col_id)
    eye_rows = row_id == col_id
    eye = lax.broadcasted_iota(jnp.int32, (width, width), 0) == lax.broadcasted_iota(
        jnp.int32, (width, width), 1
    )
    for pair in range(block):
        at = orbit_ref.shape[0] - 2 * (count_ref.shape[0] - first - pair)
        orbit, other = orbit_ref[at], orbit_ref[at + 1]
        energy = element(occ_ref, orbit, orbit) + element(occ_ref, other, other)
        energy_ref[pair] = jnp.broadcast_to(energy, (1, width))
        fock = fock_ref[pair]
        fock_rows = fock_ref[pair, pl.ds(row_start, rows), :]
        half = half_ref[pair]
        fitted = dot(left_ref[pair], right_ref[pair], 1, 1)
        put_rows(part_ref, pair, fitted + left_part(fock_rows, half))
        own_ref[pair] = dot(half, fock, 1, 0) - energy * kept_ref[pair]
        diag_cols = jnp.sum(jnp.where(eye, fock.astype(jnp.float32), 0.0), axis=0, keepdims=True)
        diag_rows = jnp.sum(
            jnp.where(eye_rows, fock_rows.astype(jnp.float32), 0.0), axis=1, keepdims=True
        )
        denominator = diag_rows + diag_cols - energy
        scale_ref[pair] = jnp.where(last < count_ref[first + pair], 1.0 / denominator, 0.0)


def any_live(read_ref, first, per_dev, rank):
    most = read_ref[first + rank]
    for item in range(rank + MOST, per_dev, MOST):
        most = jnp.maximum(most, read_ref[first + item])
    return most >= 0


def own_coef_kernel(slots, place_ref, read_ref, coef_ref, out_ref):
    per_dev = slots * MOST

    def body(turn, carry):
        far = place_ref[0] ^ (turn + 1)
        for item in range(per_dev):
            pair = jnp.maximum(read_ref[far * per_dev + item], 0)
            out_ref[turn * per_dev + item] = coef_ref[pair].T
        return carry

    lax.fori_loop(0, out_ref.shape[0] // per_dev, body, 0)


def projector_kernel(turns, place_ref, read_ref, own_ref, *rest):
    arrived, out_ref = rest[:-1], rest[-1]
    per_dev = arrived[0].shape[0]

    def rank_items(place, turn, rank):
        for item in range(rank, per_dev, MOST):
            own = own_ref[turn * per_dev + item]
            out_ref[place * per_dev + item] = dot(own, arrived[place][item], 1, 0).astype(
                jnp.bfloat16
            )

    for place, turn in enumerate(turns):
        far = place_ref[0] ^ (turn + 1)
        for rank in range(MOST):
            pl.when(any_live(read_ref, far * per_dev, per_dev, rank))(
                functools.partial(rank_items, place, turn, rank)
            )


def add_coupling(sets, place_ref, occ_ref, fetch, amps_ref, part_ref):
    parts, rows, width = part_ref.shape[0], part_ref.shape[2], part_ref.shape[3]
    per_dev = amps_ref.shape[2] // len(sets)
    slots = per_dev // MOST
    pairs = sets[0][1].shape[0] // (2 * slots + 2)
    side_at, pair_at = pairs * slots, 2 * pairs * slots

    def body(turn, place, proj_ref, read_ref, orbit_ref, offset):
        far = place_ref[0] ^ (turn + 1)
        if offset == 0:
            fetch(turn).wait()

        def rank_terms(rank):
            terms = []
            for item in range(rank, per_dev, MOST):
                pair = read_ref[far * per_dev + item]
                safe = jnp.maximum(pair, 0)
                entry = safe * slots + item // MOST
                orbit = orbit_ref[pair_at + 2 * safe + orbit_ref[side_at + entry]]
                coupled = element(occ_ref, orbit_ref[entry], orbit)
                weight = jnp.where(pair >= 0, -coupled, 0.0)
                proj = proj_ref[place * per_dev + item]
                amps = amps_ref[far, :, offset + item].reshape(width, width)
                mixed = dot(proj, amps, 1, 0).astype(jnp.bfloat16)
                terms.append((safe, weight * dot(mixed, proj, 1, 1)))
            for safe, term in terms:
                for part in range(parts):
                    part_ref[part, safe] += term[part * rows : (part + 1) * rows]

        for rank in range(MOST):
            pl.when(any_live(read_ref, far * per_dev, per_dev, rank))(
                functools.partial(rank_terms, rank)
            )

    for number, (read_ref, orbit_ref, groups) in enumerate(sets):
        for turns, proj_ref in groups:
            later = turns[min(1, len(turns) - 1)] - min(1, len(turns) - 1)

            def step(place, carry, first=turns[0], later=later, proj_ref=proj_ref):
                turn = jnp.where(place == 0, first, place + later)
                body(turn, place, proj_ref, read_ref, orbit_ref, number * per_dev)
                return carry

            lax.fori_loop(0, len(turns), step, 0)


def coupling_kernel(groups, scaled, place_ref, *refs):
    set_count = 1 if scaled else 2
    tables, refs = refs[: 2 * set_count], refs[2 * set_count :]
    occ_ref, early_ref, late_ref = refs[:3]
    sets = [(tables[0], tables[1], list(zip(groups, (early_ref, late_ref))))]
    if not scaled:
        every = tuple(range(sum(len(turns) for turns in groups)))
        sets.append((tables[2], tables[3], [(every, refs[3])]))
    amps_hbm, start_hbm, out_ref, extra_ref, amps_ref, amps_sems, start_sem, *rest = refs[
        2 + set_count :
    ]
    part_ref = out_ref if scaled else rest[0]
    parts, pairs, rows, width = start_hbm.shape
    given = amps_hbm.shape[1]
    first_row = (place_ref[1] // given) * given

    def fetch(turn):
        far = place_ref[0] ^ (turn + 1)
        return pltpu.make_async_copy(
            amps_hbm.at[far], amps_ref.at[far, pl.ds(first_row, given)], amps_sems.at[turn]
        )

    loads = [
        pltpu.make_async_copy(
            start_hbm.at[part], part_ref.at[part, pl.ds(0, pairs)], start_sem.at[part]
        )
        for part in range(parts)
    ]
    for load in loads:
        load.start()
    for turns in groups:
        for turn in turns:
            fetch(turn).start()
    if given < parts:
        blank = jnp.zeros(amps_ref.shape[2:], amps_ref.dtype)

        def clear(far, carry):
            for row in range(parts - given):
                amps_ref[far, lax.rem(first_row + given + row, parts)] = blank
            return carry

        lax.fori_loop(0, amps_ref.shape[0], clear, 0)
    for load in loads:
        load.wait()
    add_coupling(sets, place_ref, occ_ref, fetch, amps_ref, part_ref)
    if not scaled:

        def body(pair, carry):
            for part in range(parts):
                out_ref[part, pair] = part_ref[part, pair].astype(out_ref.dtype)
            extra_ref[pair] = part_ref[place_ref[1], pair]
            return carry

        lax.fori_loop(0, pairs, body, 0, unroll=4)
        return

    def body(pair, most):
        for part in range(parts):
            most = jnp.maximum(most, jnp.abs(part_ref[part, pair]))
        return most

    most = lax.fori_loop(0, pairs, body, jnp.zeros((rows, width), jnp.float32), unroll=4)
    most = jnp.max(jnp.max(most, axis=0, keepdims=True), axis=1, keepdims=True)
    power = jnp.maximum(jnp.ceil(jnp.log2(jnp.maximum(most, 1.0)) - 15.0), 0.0)
    for part in range(parts):
        out_ref[part, pairs] = jnp.broadcast_to(power * jnp.exp2(power), (rows, width))
    extra_ref[...] = jnp.broadcast_to(jnp.exp2(-power), (1, width))


def first_update_kernel(
    send_ref, sum_ref, own_ref, scale_ref, kept_ref, new_ref, half_ref, out_ref, held, sems
):
    def body(pair, carry):
        new = kept_ref[pair] - (sum_ref[pair] + own_ref[pair]) * scale_ref[pair]
        new_ref[pair] = new
        half_ref[pair] = new.astype(jnp.bfloat16)
        return carry

    lax.fori_loop(0, new_ref.shape[0], body, 0, unroll=4)
    pack_rows(send_ref, half_ref, out_ref, held, sems)


def between_kernel(
    place_ref, energy_ref, fock_ref, kept_ref, half_ref, before_ref, sum_ref, start_ref, old_ref,
    part_ref, own_ref,
):
    block, rows, width = kept_ref.shape
    row_start = pl.multiple_of(place_ref[1] * rows, rows)
    for pair in range(block):
        half = half_ref[pair]
        fock_rows = fock_ref[pair, pl.ds(row_start, rows), :]
        change = left_part(fock_rows, half) - left_part(fock_rows, before_ref[pair])
        for part in range(part_ref.shape[0]):
            part_ref[part, pair] = (
                start_ref[part, pair] - old_ref[part, pair] + change[part * rows : (part + 1) * rows]
            )
        own_ref[pair] = (
            dot(half, fock_ref[pair], 1, 0)
            - energy_ref[pair] * kept_ref[pair]
            + sum_ref[pair]
        )


def last_update_kernel(place_ref, got_ref, mine_ref, own_ref, scale_ref, kept_ref, new_ref):
    def body(pair, carry):
        total = mine_ref[pair]
        for turn in range(1, got_ref.shape[0]):
            part = lax.rem(place_ref[1] + turn, got_ref.shape[0])
            total = total + got_ref[part, pair].astype(jnp.float32)
        new_ref[pair] = kept_ref[pair] - (total + own_ref[pair]) * scale_ref[pair]
        return carry

    lax.fori_loop(0, new_ref.shape[0], body, 0, unroll=4)


def shape(dims, dtype):
    return jax.ShapeDtypeStruct(tuple(dims), dtype)


def per_device(
    pair_orbits,
    pno_count,
    partner,
    couple_orbit,
    couple_side,
    occ_fock,
    fit_left,
    fit_right,
    pno_coef,
    virt_fock,
    amps_in,
):
    pair_dev = pno_count.shape[0]
    width = virt_fock.shape[1]
    rows = amps_in.shape[1]
    slots = partner.shape[1]
    dev_count = lax.axis_size("pairs")
    aux_count = lax.axis_size("aux")
    all_slots = slots * aux_count
    per_dev = slots * MOST
    items = (dev_count - 1) * per_dev
    bf16, f32 = jnp.bfloat16, jnp.float32
    place = jnp.stack([lax.axis_index("pairs"), lax.axis_index("aux")]).astype(jnp.int32)

    orbits = [couple_orbit.reshape(-1), couple_side.reshape(-1), pair_orbits.reshape(-1)]
    orbits = jnp.concatenate(orbits)
    coef_send, coef_read = pair_places(partner, pair_dev, dev_count, True)

    def packed_coef(send):
        return pl.pallas_call(
            functools.partial(coef_kernel, slots),
            out_shape=tuple(
                shape((per_dev,) + pno_coef.shape[1:], bf16) for _ in range(dev_count - 1)
            ),
            in_specs=[SMEM, SMEM, HBM],
            out_specs=tuple(HBM for _ in range(dev_count - 1)),
            scratch_shapes=[
                pltpu.VMEM((items,) + pno_coef.shape[1:], bf16),
                pltpu.SemaphoreType.DMA((items,)),
                pltpu.SemaphoreType.DMA((dev_count - 1,)),
            ],
            compiler_params=params(shape((items,) + pno_coef.shape[1:], bf16)),
            cost_estimate=FREE,
            name="pack_coef",
        )(place, send, pno_coef)

    def sent_coef(coef_out):
        return [
            lax.ppermute(packed, "pairs", [(dev, dev ^ (turn + 1)) for dev in range(dev_count)])
            for turn, packed in enumerate(coef_out)
        ]

    coef_out = packed_coef(coef_send)
    tables = partner
    coef_far = sent_coef(coef_out)
    half_count = aux_count // 2
    more = jnp.concatenate([tables, couple_orbit, couple_side], axis=1)
    shares = [tables]
    for turn in range(1, aux_count):
        turned = [(dev, (dev + turn) % aux_count) for dev in range(aux_count)]
        shares.append(lax.ppermute(more if turn == half_count else tables, "aux", turned))
    other = shares[half_count][:, slots:]
    shares[half_count] = shares[half_count][:, :slots]
    tables = jnp.zeros((aux_count,) + tables.shape, jnp.int32)
    owners = jnp.arange(aux_count)[:, None, None]
    for turn, share in enumerate(shares):
        owner = lax.rem(place[1] + aux_count - turn, aux_count)
        tables = jnp.where(owners == owner, share[None], tables)
    tables = tables.transpose(1, 0, 2).reshape(pair_dev, all_slots)
    send = pair_places(tables, pair_dev, dev_count, False)

    other_orbits = [other[:, :slots].reshape(-1), other[:, slots:].reshape(-1)]
    other_orbits = jnp.concatenate(other_orbits + [pair_orbits.reshape(-1)])
    other_send, other_read = pair_places(shares[half_count], pair_dev, dev_count, True)
    lower = [part for dev in range(half_count) for part in (dev, dev + half_count)]
    upper = [part for dev in range(half_count) for part in (dev + half_count, dev)]
    by_part = send.reshape(dev_count, aux_count, per_dev)
    half_send = jnp.where(
        place[1] < half_count,
        jnp.stack([by_part[:, part] for part in lower], axis=1),
        jnp.stack([by_part[:, part] for part in upper], axis=1),
    ).reshape(-1)

    places = dev_count * all_slots * MOST
    packed = shape((places, rows, width), bf16)
    pack_scratch = [pltpu.VMEM(packed.shape, bf16), pltpu.SemaphoreType.DMA((dev_count,))]
    kept, half, amps_out = pl.pallas_call(
        start_kernel,
        out_shape=(
            shape(amps_in.shape, f32),
            shape(amps_in.shape, bf16),
            packed,
        ),
        in_specs=[SMEM, SMEM, SMEM, VMEM],
        out_specs=(VMEM, VMEM, HBM),
        scratch_shapes=pack_scratch,
        compiler_params=params(amps_in, amps_in, amps_in, packed),
        cost_estimate=FREE,
        name="mask_and_pack",
    )(place, send, pno_count, amps_in)

    def exchange(packed):
        packed = packed.reshape(dev_count * aux_count, per_dev, rows, width)
        got = lax.all_to_all(packed, ("pairs", "aux"), split_axis=0, concat_axis=0, tiled=True)
        return got.reshape(dev_count, aux_count, per_dev, rows, width)

    ahead = slice(1, dev_count // 2 + 1)
    leading = slice(1, dev_count // 2 + 1, 2)
    amps_out, coef_far[leading] = lax.optimization_barrier((amps_out, coef_far[leading]))
    amps_far = exchange(amps_out)

    block = 8
    by_pair = lambda *dims: pl.BlockSpec((block,) + dims, lambda step: (step,) + (0,) * len(dims))
    fit = fit_left.shape[2]
    wide = by_pair(width, width)
    slab = by_pair(rows, width)
    line = by_pair(1, width)
    tall = pl.BlockSpec((aux_count, block, rows, width), lambda step: (0, step, 0, 0))
    by_rows = shape((aux_count, pair_dev, rows, width), f32)
    start, scale, mine, energy = pl.pallas_call(
        prepare_kernel,
        grid=(pair_dev // block,),
        out_shape=(
            by_rows,
            shape(amps_in.shape, f32),
            shape(amps_in.shape, f32),
            shape((pair_dev, 1, width), f32),
        ),
        in_specs=[SMEM, SMEM, SMEM, VMEM, by_pair(width, fit), by_pair(width, fit), wide, slab, slab],
        out_specs=(tall, slab, slab, line),
        compiler_params=pltpu.CompilerParams(vmem_limit_bytes=WIDE_BYTES),
        cost_estimate=FREE,
        name="integrals",
    )(place, pno_count, orbits, occ_fock, fit_left, fit_right, virt_fock, kept, half)

    own_shape = shape((items, width, pno_coef.shape[1]), bf16)

    def own_coef(read):
        return pl.pallas_call(
            functools.partial(own_coef_kernel, slots),
            out_shape=own_shape,
            in_specs=[SMEM, SMEM, VMEM],
            out_specs=VMEM,
            compiler_params=params(pno_coef, own_shape),
            name="own_coef",
        )(place, read, pno_coef)

    def projected(turns, read, own, arrived):
        out = shape((len(turns) * per_dev, width, width), bf16)
        return pl.pallas_call(
            functools.partial(projector_kernel, turns),
            out_shape=out,
            in_specs=[SMEM, SMEM] + [VMEM] * (1 + len(turns)),
            out_specs=VMEM,
            compiler_params=params(own, out, *arrived),
            name="projectors",
        )(place, read, own, *arrived)

    early = tuple(range(dev_count - 1)[ahead])
    groups = (early, tuple(turn for turn in range(dev_count - 1) if turn not in early))
    own = own_coef(coef_read)
    projectors = [
        projected(turns, coef_read, own, [coef_far[turn] for turn in turns]) for turns in groups
    ]

    def coupled(amps_far, start, tables, projectors, scaled):
        if scaled:
            out, extra = shape((aux_count, pair_dev + 1, rows, width), f32), shape((1, width), f32)
        else:
            out, extra = shape(start.shape, bf16), shape(amps_in.shape, f32)
        held = shape((dev_count, aux_count) + amps_far.shape[2:], bf16)
        return pl.pallas_call(
            functools.partial(coupling_kernel, groups, scaled),
            out_shape=(out, extra),
            in_specs=[SMEM] * (1 + len(tables)) + [VMEM] * (1 + len(projectors)) + [HBM] * 2,
            out_specs=(VMEM, VMEM),
            scratch_shapes=[
                pltpu.VMEM(held.shape, bf16),
                pltpu.SemaphoreType.DMA((dev_count - 1,)),
                pltpu.SemaphoreType.DMA((aux_count,)),
            ]
            + ([] if scaled else [pltpu.VMEM(start.shape, f32)]),
            compiler_params=params(out, amps_in, start, held, *projectors),
            name="coupling",
        )(place, *tables, occ_fock, *projectors, amps_far, start)

    tables = [coef_read, orbits]
    total, shrink = coupled(amps_far, start, tables, projectors, True)
    to_sum = (total * shrink).astype(jnp.float16)
    to_sum, other_send = lax.optimization_barrier((to_sum, other_send))
    other_out = list(packed_coef(other_send))
    other_far = [None] * len(other_out)

    def send_turns(turns):
        for turn in turns:
            pairs = [(dev, dev ^ (turn + 1)) for dev in range(dev_count)]
            other_far[turn] = lax.ppermute(other_out[turn], "pairs", pairs)

    first, second = groups
    send_turns(first)
    tied = ([other_out[turn] for turn in second], [other_far[turn] for turn in first])
    waiting, arrived = lax.optimization_barrier(tied)
    for turn, packed_turn in zip(second, waiting):
        other_out[turn] = packed_turn
    for turn, arrived_turn in zip(first, arrived):
        other_far[turn] = arrived_turn
    send_turns(second)
    got = lax.all_to_all(to_sum, "aux", split_axis=0, concat_axis=0, tiled=True)
    foreign = (jnp.arange(aux_count) != place[1])[:, None, None, None]
    grow = jnp.where(foreign, jnp.exp2(got[:, pair_dev:, :1].astype(f32)), 0.0)
    sums = lax.dynamic_index_in_dim(total, place[1], 0, keepdims=False)[:pair_dev]
    for turn in range(aux_count):
        sums = sums + got[turn, :pair_dev].astype(f32) * grow[turn]

    every = tuple(range(dev_count - 1))
    sums, other_far = lax.optimization_barrier((sums, other_far))
    other_projectors = projected(every, other_read, own_coef(other_read), other_far)

    before = half
    kept, half, amps_out = pl.pallas_call(
        first_update_kernel,
        out_shape=(
            shape(amps_in.shape, f32),
            shape(amps_in.shape, bf16),
            packed,
        ),
        in_specs=[SMEM] + [VMEM] * 4,
        out_specs=(VMEM, VMEM, HBM),
        scratch_shapes=pack_scratch,
        compiler_params=params(amps_in, amps_in, amps_in, amps_in, amps_in, amps_in, packed),
        name="first_update",
    )(half_send, sums, mine, scale, kept)

    halves = [
        [dev * aux_count + part for dev in range(dev_count) for part in range(first, last)]
        for first, last in ((0, half_count), (half_count, aux_count))
    ]
    amps_far = amps_out.reshape(dev_count * half_count, 2 * per_dev, rows, width)
    amps_far = lax.all_to_all(
        amps_far, ("pairs", "aux"), split_axis=0, concat_axis=0, axis_index_groups=halves, tiled=True
    ).reshape(dev_count, half_count, 2 * per_dev, rows, width)

    start, own = pl.pallas_call(
        between_kernel,
        grid=(pair_dev // block,),
        out_shape=(by_rows, shape(amps_in.shape, f32)),
        in_specs=[SMEM, line, wide, slab, slab, slab, slab, tall, tall],
        out_specs=(tall, slab),
        compiler_params=params(*[shape((2 * block,) + dims, f32) for dims in ((width, 3 * width), (rows, 6 * width))]),
        cost_estimate=pl.CostEstimate(
            flops=6 * pair_dev * width * width * rows,
            bytes_accessed=pair_dev * width * width * 10,
            transcendentals=0,
        ),
        name="between",
    )(place, energy, virt_fock, kept, half, before, sums, start, total)

    tables += [other_read, other_orbits]
    projectors.append(other_projectors)
    to_sum, mine = coupled(amps_far, start, tables, projectors, False)
    got = lax.all_to_all(to_sum, "aux", split_axis=0, concat_axis=0, tiled=True)

    return pl.pallas_call(
        last_update_kernel,
        out_shape=shape(amps_in.shape, f32),
        in_specs=[SMEM] + [VMEM] * 5,
        out_specs=VMEM,
        compiler_params=params(got, mine, own, scale, kept, amps_in),
        name="last_update",
    )(place, got, mine, own, scale, kept)


def solution(mesh):
    return jax.shard_map(
        per_device,
        mesh=mesh,
        in_specs=(
            P("pairs", None),
            P("pairs"),
            P("pairs", "aux"),
            P("pairs", "aux"),
            P("pairs", "aux"),
            P(),
            P("pairs", None, "aux"),
            P("pairs", None, "aux"),
            P("pairs", None, None),
            P("pairs", None, None),
            P("pairs", "aux", None),
        ),
        out_specs=P("pairs", "aux", None),
        check_vma=False,
    )
```
